512 devices in a mesh: section: 16 (over z), kv: 8 (over x, core), tp: 4 (over y).
Axes of the slice: x: 4, y: 4, z: 16, core: 2. Of those that a mesh axis runs over, the one named last changes fastest.
Arguments:
- arriving: bfloat16 [16, 128, 4096], P('section', None, ('kv', 'tp')), may hold values from -24 to 24
- entering: bfloat16 [1, 128, 4096], P(None, None, ('kv', 'tp')), may hold values from -6 to 6
- gain_attention: float32 [16, 4096], P('section'), may hold values from 0.1 to 1.9
- gain_key: float32 [16, 4096], P('section'), may hold values from -2 to 2
- decay_rate: float32 [16, 32], P('section', ('kv', 'tp')), may hold values from 0.001953125 to 0.06
- state_in: float32 [16, 32, 128, 128], P('section', ('kv', 'tp')), may hold values from -4 to 4
- gain_linear: float32 [16, 4096], P('section', ('kv', 'tp')), may hold values from 0.1 to 1.9
- gain_feed: float32 [16, 4096], P('section'), may hold values from 0.1 to 1.9
- gate_up: bfloat16 [16, 4608, 2, 4096], P('section', ('kv', 'tp')), may hold values from -0.09375 to 0.09375
- down_weight: bfloat16 [16, 4608, 4096], P('section', ('kv', 'tp')), may hold values from -0.15625 to 0.15625
- prefix_keys: bfloat16 [16, 512, 8, 512], P('section', 'kv', None, 'tp'), may hold values from -1500 to 1500
- prefix_values: bfloat16 [16, 512, 8, 512], P('section', 'kv', None, 'tp'), may hold values from -6 to 6
- lengths: int32 [16, 8], P('section'), may hold values from 1 to 64, 288 in all within a row
Outputs:
- arrived: bfloat16 [2, 16, 128, 4096], P(None, 'section', None, ('kv', 'tp'))
- state_out: float32 [16, 32, 128, 128], P('section', ('kv', 'tp'))
The draws below stay inside these ranges and needn't reach their ends.
Inputs may be any that keep to these rules, and one draw needn't show every extreme that they name: `lengths`: in every section one shard is full (64 rows).
All inputs are finite; a program needn't handle non-finite values.
Results may differ from the reference program's by a relative error of at most 0.025.
Values may be sent and summed in bfloat16 or wider, within the bound.
No kernel may reach another device: no remote copies, remote signals or barrier semaphores. Data moves between devices by JAX's collectives and lax.ppermute only.
A program may use at most 64 MiB of HBM per device.

```python
import math
from functools import partial
import jax
import jax.numpy as jnp
import numpy as np
from jax import lax

H = 32
HEAD = 128
FF = 4608
TOK_MC = 128
P_DEV = 64
TICKS = 2
D = 4096
SECTIONS = 16
PREFIX = 512
N_KV = 8
N_TP = 4


def shared_rows(key):
    first = jax.random.fold_in(key, 0)
    third = jax.random.fold_in(key, 2)
    fourth = jax.random.fold_in(key, 3)
    gauss = jnp.clip(jax.random.normal(first, (SECTIONS, TOK_MC, D), jnp.float32), -4.0, 4.0)
    column_scale = jnp.exp(jax.random.uniform(third, (D,), jnp.float32, -1.2, 1.1))
    row_scale = jnp.exp(jax.random.uniform(fourth, (SECTIONS, TOK_MC, 1), jnp.float32, -0.7, 0.7))
    return gauss * column_scale * row_scale


def draw_arriving(key, part):
    return shared_rows(key).astype(jnp.bfloat16)


def draw_prefix_keys(key, part):
    key = jax.random.fold_in(key, 11)
    shards = PREFIX // P_DEV
    base = jnp.clip(jax.random.normal(key, (SECTIONS, PREFIX, D), jnp.float32), -4.0, 4.0)
    return base.reshape(SECTIONS, PREFIX, shards, D // shards).astype(jnp.bfloat16)


def raised(result, stream_key, source, target, shards_of, factor):
    owner, partner = [(jnp.arange(result.shape[position]) // (result.shape[position] // shards_of)).reshape([-1 if axis == position else 1 for axis in range(result.ndim)]) for position in (source, target)]
    chosen = jax.random.permutation(stream_key, shards_of)[partner]
    strong = (owner == chosen) | (owner == (partner + shards_of // 2) % shards_of)
    return jnp.where(strong, factor * result, result)


def shard_levels(rng, shape, pieces, least, high):
    def one(position, parts):
        steps = jax.random.uniform(jax.random.fold_in(jax.random.fold_in(rng, 6), position), (parts,), jnp.float32, least / len(pieces), high / len(pieces))
        return jnp.repeat(jnp.exp(steps), shape[position] // parts).reshape((-1,) + (1,) * (len(shape) - position - 1))

    gain = one(*pieces[0])
    for cut in pieces[1:]:
        gain = gain * one(*cut)
    return gain


def length_profile(amount, total, limit, skew):
    loads = [(1 << 20) // math.isqrt(rank ** skew) + 1 for rank in range(2, amount + 1)]
    spare, given = total - limit - (amount - 1), [1] * (amount - 1)
    while spare > 0:
        movable = [i for i in range(amount - 1) if given[i] < limit]
        pool, left = sum([loads[i] for i in movable]), spare
        for i in movable:
            addition = min(limit - given[i], max(1, left * loads[i] // pool), spare)
            given[i] = given[i] + addition
            spare = spare - addition
    return np.array([limit] + given)


def uneven(key, count, total, reach, slope):
    if count == 2:
        one = jax.random.randint(key, (), max(1, total - reach), min(reach, total - 1) + 1)
        return jnp.stack([one, total - one])
    sizes = jnp.asarray(length_profile(count, total, reach, slope), jnp.int32)
    twos = (count - 1) // 2
    source_of, receiver = sizes[1:1 + 2 * twos:2], sizes[2:2 + 2 * twos:2]
    slack = jnp.minimum(source_of - 1, reach - receiver)
    passed = jax.random.randint(jax.random.fold_in(key, 1), (twos,), 0, 1 << 20) % (slack + 1)
    sizes = sizes.at[1:1 + 2 * twos:2].set(source_of - passed).at[2:2 + 2 * twos:2].set(receiver + passed)
    return sizes[jax.random.permutation(jax.random.fold_in(key, 2), count)]


def normal_values(stream_key, shape, width, most, cuts=(), held_as=jnp.bfloat16):
    result = width * jax.random.normal(stream_key, shape, jnp.float32)
    if cuts:
        result = result * shard_levels(stream_key, shape, cuts, -0.22, 0.18)
    return jnp.clip(result, -most, most).astype(held_as)


def noise_with(own_key, dims, width, limit, cuts, heavy, kind=jnp.bfloat16):
    values = width * jax.random.normal(own_key, dims, jnp.float32)
    if cuts:
        values = values * shard_levels(own_key, dims, cuts, -0.22, 0.18)
    return jnp.clip(raised(values, jax.random.fold_in(own_key, 3), *heavy), -limit, limit).astype(kind)


def setup_inputs(seed: int = 0) -> dict:
    streams_of = jax.random.split(jax.random.key(seed), 14)
    arriving = draw_arriving(jax.random.fold_in(streams_of[13], 71), 0)
    entering = normal_values(streams_of[1], (TICKS - 1, TOK_MC, D), 1.0, 6.0, ((2, 32),))
    gain_attention = jnp.clip(1.0 + 0.18 * jax.random.normal(streams_of[2], (SECTIONS, D), jnp.float32), 0.1, 1.9)
    gain_key = jnp.clip(jax.random.uniform(streams_of[3], (SECTIONS, D), jnp.float32, -2.0, 2.0) * shard_levels(streams_of[3], (SECTIONS, D), ((0, 16),), -0.4, 0.0), -2.0, 2.0)
    decay_rate = jnp.clip(jnp.exp(math.log(0.06) - 3.424914 * jax.random.uniform(streams_of[4], (SECTIONS, H), jnp.float32) ** shard_levels(streams_of[4], (SECTIONS, H), ((0, 16), (1, 32)), -0.2, 0.2)), 0.001953125, 0.06)
    state_in = normal_values(streams_of[5], (SECTIONS, H, HEAD, HEAD), 0.5, 4.0, ((0, 16), (1, 32)), jnp.float32)
    gain_linear = jnp.clip(1.0 + 0.18 * jax.random.normal(streams_of[6], (SECTIONS, D), jnp.float32), 0.1, 1.9)
    gain_feed = jnp.clip(1.0 + 0.18 * jax.random.normal(streams_of[7], (SECTIONS, D), jnp.float32), 0.1, 1.9)
    gate_up = normal_values(streams_of[8], (SECTIONS, FF, 2, D), D ** -0.5, 0.09375, ((0, 16), (1, 32)))
    down_weight = noise_with(streams_of[9], (SECTIONS, FF, D), FF ** -0.5, 0.15625, ((0, 16), (1, 32)), (1, 2, 32, 2.75))
    prefix_keys = draw_prefix_keys(jax.random.fold_in(streams_of[13], 71), 0)
    prefix_values = normal_values(streams_of[11], (SECTIONS, PREFIX, N_KV, D // N_KV), 1.0, 6.0, ((0, 16), (1, 8), (3, 4)))
    lengths = jax.vmap(lambda own: uneven(own, N_KV, N_KV * P_DEV // 2 + P_DEV // 2, P_DEV, 2))(jax.random.split(streams_of[12], SECTIONS)).reshape((SECTIONS, N_KV)).astype(jnp.int32)
    return dict(arriving=arriving, entering=entering, gain_attention=gain_attention, gain_key=gain_key, decay_rate=decay_rate, state_in=state_in, gain_linear=gain_linear, gain_feed=gain_feed, gate_up=gate_up, down_weight=down_weight, prefix_keys=prefix_keys, prefix_values=prefix_values, lengths=lengths)


def rms_scale(values):
    return lax.rsqrt(lax.optimization_barrier(jnp.mean(values * values, axis=-1, keepdims=True)) + 1e-06)

def lightning(head_queries, head_keys, head_values, decays, memory):
    tokens = head_queries.shape[0]
    head_size = head_queries.shape[2]
    positions = jnp.arange(tokens).astype(jnp.float32)
    distance = positions[:, None] - positions[None, :]
    causal = distance >= 0.0
    decay_mask = jnp.exp(-decays[:, None, None] * jnp.where(causal, distance, 0.0)[None])
    decay_mask = jnp.where(causal[None], decay_mask, 0.0)
    scores = jnp.einsum('thc,shc->hts', head_queries.astype(jnp.float32), head_keys.astype(jnp.float32))
    weights = (scores * decay_mask * head_size ** (-0.5)).astype(jnp.bfloat16)
    within = jnp.einsum('hts,shc->thc', weights.astype(jnp.float32), head_values.astype(jnp.float32))
    carry_scale = jnp.exp(-decays[None, :] * (positions[:, None] + 1.0))
    carried = jnp.einsum('thc,hce->the', head_queries.astype(jnp.float32), memory, precision=lax.Precision.HIGHEST) * carry_scale[:, :, None]
    tail_scale = jnp.exp(-decays[None, :] * (tokens - 1.0 - positions[:, None]))
    update = jnp.einsum('shc,she->hce', head_keys.astype(jnp.float32) * tail_scale[:, :, None], head_values.astype(jnp.float32), precision=lax.Precision.HIGHEST)
    new_memory = memory * jnp.exp(-decays * tokens)[:, None, None] + update * head_size ** (-0.5)
    return (within + carried, new_memory)

def attend(head_queries, all_keys, all_values, allowed):
    head_size = head_queries.shape[2]
    scores = jnp.einsum('thc,khc->htk', head_queries.astype(jnp.float32), all_keys.astype(jnp.float32))
    scores = jnp.where(allowed[None], scores * head_size ** (-0.5), -1e+30)
    row_max = lax.optimization_barrier(jnp.max(scores, axis=-1))
    probabilities = jnp.where(allowed[None], jnp.exp(scores - row_max[..., None]), 0.0)
    row_sum = lax.optimization_barrier(jnp.sum(probabilities, axis=-1))
    weighted = jnp.einsum('htk,khc->htc', probabilities.astype(jnp.bfloat16).astype(jnp.float32), all_values.astype(jnp.float32))
    return (row_max, row_sum, weighted)

def section_layer(packed, tick_index):
    rows_in, attention_gain, key_gain, decays, memory, linear_gain, feed_gain, weights_in, weights_out, keys_before, values_before, valid_count, earlier = packed
    tokens = rows_in.shape[0]
    widened = rows_in.astype(jnp.float32)
    normed = widened * rms_scale(widened) * attention_gain
    queries = normed.astype(jnp.bfloat16)
    key_rows = (normed * key_gain).astype(jnp.bfloat16)
    head_queries = queries.reshape(tokens, H, HEAD)
    head_keys = key_rows.reshape(tokens, H, HEAD)
    lin_raw, memory = lightning(head_queries, head_keys, head_queries, decays, memory)
    linear = lin_raw * rms_scale(lin_raw) * linear_gain.reshape(H, HEAD)
    own_keys = head_keys
    own_values = head_queries
    if earlier is not None:
        own_keys = jnp.concatenate([earlier[0], head_keys], axis=0)
        own_values = jnp.concatenate([earlier[1], head_queries], axis=0)
    all_keys = jnp.concatenate([keys_before.reshape(PREFIX, H, HEAD), own_keys], axis=0)
    all_values = jnp.concatenate([values_before.reshape(PREFIX, H, HEAD), own_values], axis=0)
    prefix_slot = jnp.arange(PREFIX)
    prefix_used = prefix_slot % P_DEV < valid_count[prefix_slot // P_DEV]
    row_place = tick_index * tokens + jnp.arange(tokens)
    own_place = jnp.arange(own_keys.shape[0])
    allowed = jnp.concatenate([jnp.broadcast_to(prefix_used[None], (tokens, PREFIX)), own_place[None, :] <= row_place[:, None]], axis=1)
    row_max, row_sum, weighted = attend(head_queries, all_keys, all_values, allowed)
    softmax_out = jnp.transpose(weighted / row_sum[..., None], (1, 0, 2))
    mixed_in = (widened + (linear + softmax_out).reshape(tokens, -1)).astype(jnp.bfloat16)
    mixed_wide = mixed_in.astype(jnp.float32)
    feed_in = (mixed_wide * rms_scale(mixed_wide) * feed_gain).astype(jnp.bfloat16)
    gate_out = jnp.dot(feed_in, jnp.transpose(weights_in[:, 0, :]), preferred_element_type=jnp.float32)
    up_out = jnp.dot(feed_in, jnp.transpose(weights_in[:, 1, :]), preferred_element_type=jnp.float32)
    hidden = (jax.nn.silu(gate_out) * up_out).astype(jnp.bfloat16)
    groups = N_KV * N_TP
    hidden_groups = jnp.transpose(hidden.reshape(tokens, groups, FF // groups), (1, 0, 2))
    weight_groups = weights_out.reshape(groups, FF // groups, D)

    def add_group(running, pair):
        piece = jnp.dot(pair[0], pair[1], preferred_element_type=jnp.float32).astype(jnp.bfloat16)
        return (running + piece.astype(jnp.float32), None)
    down_sum, _ = lax.scan(add_group, jnp.zeros((tokens, D), jnp.float32), (hidden_groups, weight_groups))
    finished = (mixed_wide + down_sum).astype(jnp.bfloat16)
    return (finished, memory, head_keys, head_queries)

def reference(arriving, entering, gain_attention, gain_key, decay_rate, state_in, gain_linear, gain_feed, gate_up, down_weight, prefix_keys, prefix_values, lengths):
    current = arriving
    memory = state_in
    past_keys = []
    past_values = []
    arrived = []
    finished = arriving
    for tick_index in range(TICKS):
        if tick_index > 0:
            current = jnp.concatenate([entering[tick_index - 1][None], finished[:-1]], axis=0)
        earlier = None
        if tick_index > 0:
            earlier = (jnp.concatenate(past_keys, axis=1), jnp.concatenate(past_values, axis=1))
        packed = (current, gain_attention, gain_key, decay_rate, memory, gain_linear, gain_feed, gate_up, down_weight, prefix_keys, prefix_values, lengths, earlier)
        finished, memory, key_rows, value_rows = lax.map(partial(section_layer, tick_index=tick_index), packed)
        past_keys.append(key_rows)
        past_values.append(value_rows)
        arrived.append(jnp.roll(finished, 1, axis=0))
    return (jnp.stack(arrived), memory)
```

```python
import functools

import jax
import jax.numpy as jnp
from jax import lax
from jax.experimental import pallas as pl
from jax.experimental.pallas import tpu as pltpu
from jax.sharding import PartitionSpec as P

TICKS = 2
TOK = 128
HALF = 64
HEAD = 128
DIM = 4096
UNITS = 144
BLOCKS = 32
SHARDS = 8
ROWS = 64
EPS = 1e-6
SECTION = ("x", "core", "tp")
F32 = jnp.float32
BF16 = jnp.bfloat16
HIGH = lax.Precision.HIGHEST


def dot(left, right, dims, precision=None):
    return lax.dot_general(
        left, right, ((dims[:1], dims[1:]), ((), ())), precision=precision, preferred_element_type=F32
    )


def block_place():
    return (lax.axis_index("x") * 2 + lax.axis_index("core")) * 4 + lax.axis_index("tp")


def write_square_sums(rows, parts_ref):
    squares = rows.astype(F32)
    squares = squares * squares
    sums = dot(jnp.ones((8, HEAD), F32), squares, (1, 1), HIGH)
    parts_ref[...] = jnp.concatenate([sums] * (BLOCKS // 8), axis=0)


def first_squares_kernel(rows_ref, parts_ref):
    write_square_sums(rows_ref[...], parts_ref)


def later_squares_kernel(passed_ref, entering_ref, rows_ref, parts_ref):
    rows = jnp.where(lax.axis_index("section") == 0, entering_ref[...], passed_ref[...])
    rows_ref[...] = rows
    write_square_sums(rows, parts_ref)


def attention_kernel(
    tick,
    lengths_ref,
    decay_ref,
    rows_ref,
    parts_ref,
    gain_ref,
    key_gain_ref,
    linear_gain_ref,
    memory_ref,
    prefix_ref,
    past_ref,
    spread_ref,
    mixed_ref,
    new_memory_ref,
    turn_ref,
):
    scale = HEAD**-0.5
    place = pl.ds(pl.multiple_of(block_place() * HEAD, HEAD), HEAD)
    sums = dot(parts_ref[...], jnp.ones((BLOCKS, HEAD), F32), (0, 0), HIGH)
    rows = rows_ref[...].astype(F32)
    normed = rows * lax.rsqrt(sums * (1.0 / DIM) + EPS) * gain_ref[:, place]
    queries = normed.astype(BF16)
    keys = (normed * key_gain_ref[:, place]).astype(BF16)
    turn_ref[0] = keys
    turn_ref[1] = queries

    decay = decay_ref[0, 0]
    shape = (TOK, TOK)
    row = lax.broadcasted_iota(jnp.int32, shape, 0)
    column = lax.broadcasted_iota(jnp.int32, shape, 1)
    causal = column <= row
    own_scores = dot(queries, keys, (1, 1)) * scale
    age = jnp.where(causal, row - column, 0).astype(F32)
    weights = jnp.where(causal, own_scores * jnp.exp(-decay * age), 0.0).astype(BF16)
    row = row.astype(F32)
    memory = memory_ref[...]
    wide = queries.astype(F32)
    raw = dot(weights, queries, (1, 0)) + dot(wide, memory, (1, 0), HIGH) * jnp.exp(
        -decay * (row + 1.0)
    )
    tail = keys.astype(F32) * jnp.exp(-decay * (TOK - 1.0 - row))
    new_memory_ref[...] = memory * jnp.exp(jnp.full(shape, -decay * TOK, F32)) + (
        dot(tail, wide, (0, 0), HIGH) * scale
    )
    spread = jnp.mean(raw * raw, axis=1, keepdims=True)
    linear = raw * lax.rsqrt(spread + EPS) * linear_gain_ref[...]

    prefix_keys = prefix_ref[:, :ROWS, :].reshape(SHARDS * ROWS, HEAD)
    prefix_values = prefix_ref[:, ROWS:, :].reshape(SHARDS * ROWS, HEAD)
    slot = lax.broadcasted_iota(jnp.int32, (1, SHARDS * ROWS), 1)
    used = jnp.zeros((1, SHARDS * ROWS), jnp.int32)
    for shard in range(SHARDS):
        used = jnp.where(slot // ROWS == shard, lengths_ref[0, shard], used)
    prefix_scores = jnp.where(
        slot % ROWS < used, dot(queries, prefix_keys, (1, 1)) * scale, -1e30
    )
    groups = [
        (prefix_scores, prefix_values),
        (jnp.where(causal, own_scores, -1e30), queries),
    ]
    if tick:
        groups.append((dot(queries, past_ref[0], (1, 1)) * scale, past_ref[1]))
    top = functools.reduce(
        jnp.maximum, [jnp.max(scores, axis=1, keepdims=True) for scores, _ in groups]
    )
    total = 0.0
    weighted = 0.0
    for scores, values in groups:
        probabilities = jnp.exp(scores - top)
        total = total + jnp.sum(probabilities, axis=1, keepdims=True)
        weighted = weighted + dot(probabilities.astype(BF16), values, (1, 0))
    mixed = (rows + (linear + weighted / total)).astype(BF16)
    mixed_ref[...] = mixed
    for block in range(BLOCKS):
        half = block // 4 % 2
        spread_ref[block] = mixed[half * HALF : (half + 1) * HALF]


def feed_kernel(rows_ref, gain_ref, near_ref, far_ref, out_ref, feed_ref, wide_ref):
    squares = jnp.zeros((HALF, HEAD), F32)
    for block in range(BLOCKS):
        place = slice(block * HEAD, (block + 1) * HEAD)
        rows = rows_ref[block].astype(F32)
        squares = squares + rows * rows
        feed_ref[:, place] = (rows * gain_ref[:, place]).astype(BF16)
    sums = dot(jnp.ones((8, HEAD), F32), squares, (1, 1), HIGH)[:1]
    factor = lax.rsqrt(sums * (1.0 / DIM) + EPS)
    wide_ref[...] = jnp.zeros_like(wide_ref)
    step = 512

    @pl.loop(0, DIM // step)
    def _(chunk):
        place = pl.ds(pl.multiple_of(chunk * step, step), step)
        feed = feed_ref[:, place]
        for side, ref in enumerate((near_ref, far_ref)):
            wide_ref[side] += dot(ref[: 2 * UNITS, place], feed, (1, 1))

    hidden = []
    for side in range(2):
        gate = wide_ref[side, :UNITS] * factor
        up = wide_ref[side, UNITS:] * factor
        hidden.append((gate / (1.0 + jnp.exp(-gate)) * up).astype(BF16))

    for chunk in range(DIM // step):
        place = slice(chunk * step, (chunk + 1) * step)
        down = dot(hidden[0], near_ref[2 * UNITS :, place], (0, 0)) + dot(
            hidden[1], far_ref[2 * UNITS :, place], (0, 0)
        )
        for block in range(step // HEAD):
            out_ref[chunk * (step // HEAD) + block] = down[
                :, block * HEAD : (block + 1) * HEAD
            ].astype(BF16)


def finish_kernel(parts_ref, mixed_ref, out_ref):
    for half in range(2):
        total = jnp.zeros((HALF, HEAD), F32)
        for block in range(BLOCKS):
            if block // 4 % 2 == half:
                total = total + parts_ref[block].astype(F32)
        place = slice(half * HALF, (half + 1) * HALF)
        out_ref[place] = (mixed_ref[place].astype(F32) + total).astype(BF16)


def shape_of(*shape, dtype=BF16):
    return jax.ShapeDtypeStruct(shape, dtype)


def local_call(kernel, outs, ins, scratch=(), scalars=0):
    vmem = pl.BlockSpec(memory_space=pltpu.VMEM)
    smem = pl.BlockSpec(memory_space=pltpu.SMEM)
    return pl.pallas_call(
        kernel,
        out_shape=outs,
        in_specs=[smem] * scalars + [vmem] * (len(ins) - scalars),
        out_specs=jax.tree.map(lambda _: vmem, outs),
        scratch_shapes=list(scratch),
        compiler_params=pltpu.CompilerParams(vmem_limit_bytes=40 * 1024 * 1024),
    )(*ins)


def swapped(value):
    return lax.ppermute(value, "core", [(0, 1), (1, 0)])


def exchanged(value, axes=SECTION):
    return lax.all_to_all(value, axes, 0, 0, tiled=True)


def per_device(
    arriving,
    entering,
    gain_attention,
    gain_key,
    decay_rate,
    state_in,
    gain_linear,
    gain_feed,
    gate_up,
    down_weight,
    prefix_keys,
    prefix_values,
    lengths,
):
    weights = jnp.concatenate([gate_up[0, :, 0], gate_up[0, :, 1], down_weight[0]], axis=0)
    far_weights = swapped(weights)
    prefix = jnp.concatenate([prefix_keys[0], prefix_values[0]], axis=0)
    prefix = exchanged(jnp.transpose(prefix, (1, 0, 2)), ("x", "core"))
    rows = arriving[0]
    memory = state_in[0, 0]
    turn = None
    arrived = []
    for tick in range(TICKS):
        if tick == 0:
            parts = local_call(first_squares_kernel, shape_of(BLOCKS, HEAD, dtype=F32), (rows,))
        else:
            rows, parts = local_call(
                later_squares_kernel,
                (shape_of(TOK, HEAD), shape_of(BLOCKS, HEAD, dtype=F32)),
                (arrived[-1], entering[tick - 1]),
            )
        parts = exchanged(parts)
        past = jnp.zeros((2, 16, HEAD), BF16) if turn is None else turn
        spread, mixed, memory, turn = local_call(
            functools.partial(attention_kernel, tick),
            (
                shape_of(BLOCKS, HALF, HEAD),
                shape_of(TOK, HEAD),
                shape_of(HEAD, HEAD, dtype=F32),
                shape_of(2, TOK, HEAD),
            ),
            (
                lengths,
                decay_rate,
                rows,
                parts,
                gain_attention,
                gain_key,
                gain_linear,
                memory,
                prefix,
                past,
            ),
            scalars=2,
        )
        spread = exchanged(spread)
        down = local_call(
            feed_kernel,
            shape_of(BLOCKS, HALF, HEAD),
            (spread, gain_feed, weights, far_weights),
            scratch=(pltpu.VMEM((HALF, DIM), BF16), pltpu.VMEM((2, 2 * UNITS, HALF), F32)),
        )
        down = exchanged(down)
        finished = local_call(finish_kernel, shape_of(TOK, HEAD), (down, mixed))
        size = lax.axis_size("section")
        arrived.append(
            lax.ppermute(finished, "section", [(i, (i + 1) % size) for i in range(size)])
        )
    return (jnp.stack(arrived)[:, None], memory[None, None])


def solution(mesh):
    shape = mesh.devices.shape
    split = jax.sharding.Mesh(
        mesh.devices.reshape(shape[0], shape[1] // 2, 2, shape[2]), ("section", "x", "core", "tp")
    )
    kv = ("x", "core")
    in_specs = (
        P("section", None, SECTION),
        P(None, None, SECTION),
        P("section", None),
        P("section", None),
        P("section", SECTION),
        P("section", SECTION, None, None),
        P("section", SECTION),
        P("section", None),
        P("section", SECTION, None, None),
        P("section", SECTION, None),
        P("section", kv, None, "tp"),
        P("section", kv, None, "tp"),
        P("section", None),
    )
    out_specs = (P(None, "section", None, SECTION), P("section", SECTION, None, None))
    return jax.shard_map(
        per_device, mesh=split, in_specs=in_specs, out_specs=out_specs, check_vma=False
    )
```

```python
import functools

import jax
import jax.numpy as jnp
from jax import lax
from jax.experimental import pallas as pl
from jax.experimental.pallas import tpu as pltpu
from jax.sharding import PartitionSpec as P

TICKS = 2
TOK = 128
HALF = 64
HEAD = 128
DIM = 4096
UNITS = 144
BLOCKS = 32
SHARDS = 8
ROWS = 64
GROUPS = 3
GROUP = UNITS // GROUPS
EPS = 1e-6
MASKED = -1e30
SECTION = ("x", "core", "tp")
F32 = jnp.float32
BF16 = jnp.bfloat16
HIGH = lax.Precision.HIGHEST


def dot(left, right, dims, precision=None):
    return lax.dot_general(
        left, right, ((dims[:1], dims[1:]), ((), ())), precision=precision, preferred_element_type=F32
    )


def block_place():
    return (lax.axis_index("x") * 2 + lax.axis_index("core")) * 4 + lax.axis_index("tp")


def write_square_sums(rows, parts_ref):
    squares = rows.astype(F32)
    squares = squares * squares
    sums = dot(jnp.ones((8, HEAD), F32), squares, (1, 1), HIGH)
    parts_ref[...] = jnp.concatenate([sums] * (BLOCKS // 8), axis=0)


def first_squares_kernel(rows_ref, parts_ref):
    write_square_sums(rows_ref[...], parts_ref)


def later_squares_kernel(passed_ref, entering_ref, rows_ref, parts_ref):
    rows = jnp.where(lax.axis_index("section") == 0, entering_ref[...], passed_ref[...])
    rows_ref[...] = rows
    write_square_sums(rows, parts_ref)


def attention_kernel(tick, decay_ref, parts_in, prefix_in, rows_in, memory_in, *refs):
    scale = HEAD**-0.5
    place = pl.ds(pl.multiple_of(block_place() * HEAD, HEAD), HEAD)
    if tick == 0:
        lengths_hbm, gain_hbm, key_gain_hbm, linear_gain_hbm = refs[:4]
        spread_ref, mixed_ref, new_memory_ref, turn_ref, consts_ref, prefix_ref = refs[4:10]
        lengths_ref, gains_ref, parts_ref, rows_ref, memory_ref, sems = refs[10:]
        copies = [
            (parts_in, parts_ref),
            (rows_in, rows_ref),
            (gain_hbm.at[:, place], gains_ref.at[0]),
            (key_gain_hbm.at[:, place], gains_ref.at[1]),
            (linear_gain_hbm, gains_ref.at[2]),
            (memory_in, memory_ref),
            (lengths_hbm, lengths_ref),
            (prefix_in, prefix_ref),
        ]
        copies = [pltpu.make_async_copy(*pair, sems.at[i]) for i, pair in enumerate(copies)]
        for copy in copies:
            copy.start()
        for copy in copies[:-1]:
            copy.wait()
        slot = lax.broadcasted_iota(jnp.int32, (1, SHARDS * ROWS), 1)
        used = jnp.zeros((1, SHARDS * ROWS), jnp.int32)
        for shard in range(SHARDS):
            used = jnp.where(slot // ROWS == shard, lengths_ref[0, shard], used)
        barred = jnp.where(slot % ROWS < used, 0.0, MASKED)
        consts_ref[0:1] = barred
        gain, key_gain, linear_gain = [gains_ref[index] for index in range(3)]
        for index in range(3):
            consts_ref[1:2, index * HEAD : (index + 1) * HEAD] = gains_ref[index]
    else:
        past_ref, consts_ref, spread_ref, mixed_ref, new_memory_ref, turn_ref = refs
        parts_ref, prefix_ref, rows_ref, memory_ref = parts_in, prefix_in, rows_in, memory_in
        barred = consts_ref[0:1]
        gain, key_gain, linear_gain = [
            consts_ref[1:2, index * HEAD : (index + 1) * HEAD] for index in range(3)
        ]
    decay = decay_ref[0, 0]
    sums = dot(parts_ref[...], jnp.ones((BLOCKS, HEAD), F32), (0, 0), HIGH)
    rows = rows_ref[...].astype(F32)
    normed = rows * lax.rsqrt(sums * (1.0 / DIM) + EPS) * gain
    queries = normed.astype(BF16)
    keys = (normed * key_gain).astype(BF16)
    turn_ref[0] = keys
    turn_ref[1] = queries

    shape = (TOK, TOK)
    row = lax.broadcasted_iota(jnp.int32, shape, 0)
    column = lax.broadcasted_iota(jnp.int32, shape, 1)
    causal = column <= row
    own_scores = dot(queries, keys, (1, 1)) * scale
    age = jnp.where(causal, row - column, 0).astype(F32)
    weights = jnp.where(causal, own_scores * jnp.exp(-decay * age), 0.0).astype(BF16)
    row = row.astype(F32)
    memory = memory_ref[...]
    wide = queries.astype(F32)
    raw = dot(weights, queries, (1, 0)) + dot(wide, memory, (1, 0), HIGH) * jnp.exp(
        -decay * (row + 1.0)
    )
    tail = keys.astype(F32) * jnp.exp(-decay * (TOK - 1.0 - row))
    new_memory_ref[...] = memory * jnp.exp(jnp.full(shape, -decay * TOK, F32)) + (
        dot(tail, wide, (0, 0), HIGH) * scale
    )
    spread = jnp.mean(raw * raw, axis=1, keepdims=True)
    linear = raw * lax.rsqrt(spread + EPS) * linear_gain

    if tick == 0:
        copies[-1].wait()
    prefix_keys = prefix_ref[:, :ROWS, :].reshape(SHARDS * ROWS, HEAD)
    prefix_values = prefix_ref[:, ROWS:, :].reshape(SHARDS * ROWS, HEAD)
    prefix_scores = dot(queries, prefix_keys, (1, 1)) * scale + barred
    groups = [
        (prefix_scores, prefix_values),
        (jnp.where(causal, own_scores, MASKED), queries),
    ]
    if tick:
        groups.append((dot(queries, past_ref[0], (1, 1)) * scale, past_ref[1]))
    top = functools.reduce(
        jnp.maximum, [jnp.max(scores, axis=1, keepdims=True) for scores, _ in groups]
    )
    total = 0.0
    weighted = 0.0
    for scores, values in groups:
        probabilities = jnp.exp(scores - top)
        total = total + jnp.sum(probabilities, axis=1, keepdims=True)
        weighted = weighted + dot(probabilities.astype(BF16), values, (1, 0))
    mixed = (rows + (linear + weighted / total)).astype(BF16)
    mixed_ref[...] = mixed
    for block in range(BLOCKS):
        half = block // 4 % 2
        spread_ref[block] = mixed[half * HALF : (half + 1) * HALF]


def feed_kernel(rows_ref, gain_ref, near_ref, far_ref, out_ref, wide_ref):
    step = 1024
    squares = jnp.zeros((HALF, HEAD), F32)
    sums = [0.0, 0.0]
    for first in range(0, DIM, step):
        place = slice(first, first + step)
        pieces = []
        for block in range(first // HEAD, (first + step) // HEAD):
            rows = rows_ref[block].astype(F32)
            squares = squares + rows * rows
            gain = gain_ref[:, block * HEAD : (block + 1) * HEAD]
            pieces.append((rows * gain).astype(BF16))
        feed = jnp.concatenate(pieces, axis=1)
        for side, ref in enumerate((near_ref, far_ref)):
            sums[side] = sums[side] + dot(ref[: 2 * UNITS, place], feed, (1, 1))
    mean = dot(jnp.ones((8, HEAD), F32), squares, (1, 1), HIGH)[:1] * (1.0 / DIM)
    factor = lax.rsqrt(mean + EPS)
    hidden = []
    for side in range(2):
        wide_ref[side] = sums[side]
        gate = wide_ref[side, pl.ds(0, UNITS, stride=2), :] * factor
        up = wide_ref[side, pl.ds(1, UNITS, stride=2), :] * factor
        hidden.append(jnp.transpose((gate / (1.0 + jnp.exp(-gate)) * up).astype(BF16)))
    for first in range(0, DIM, step):
        place = slice(first, first + step)
        down = dot(hidden[0], near_ref[2 * UNITS :, place], (1, 0)) + dot(
            hidden[1], far_ref[2 * UNITS :, place], (1, 0)
        )
        for block in range(step // HEAD):
            out_ref[first // HEAD + block] = down[:, block * HEAD : (block + 1) * HEAD].astype(BF16)


def prepare_kernel(gate_up_hbm, down_hbm, weights_ref, raw_ref, sems):
    copies = []
    for group in range(GROUPS):
        span = pl.ds(group * GROUP, GROUP)
        copies.append((gate_up_hbm.at[span], raw_ref.at[span]))
    copies.append((down_hbm, weights_ref.at[pl.ds(2 * UNITS, UNITS)]))
    copies = [pltpu.make_async_copy(*pair, sems.at[i]) for i, pair in enumerate(copies)]
    for copy in copies:
        copy.start()
    for group in range(GROUPS):
        copies[group].wait()

        @pl.loop(0, GROUP // 16)
        def _(part):
            raw = raw_ref[pl.ds(group * GROUP + part * 16, 16)]
            target = pl.ds(pl.multiple_of(2 * group * GROUP + part * 32, 32), 32)
            weights_ref[target] = raw.reshape(32, DIM)

    copies[GROUPS].wait()


def finish_kernel(parts_ref, mixed_ref, out_ref):
    for half in range(2):
        total = jnp.zeros((HALF, HEAD), F32)
        for block in range(BLOCKS):
            if block // 4 % 2 == half:
                total = total + parts_ref[block].astype(F32)
        place = slice(half * HALF, (half + 1) * HALF)
        out_ref[place] = (mixed_ref[place].astype(F32) + total).astype(BF16)


def shape_of(*shape, dtype=BF16):
    return jax.ShapeDtypeStruct(shape, dtype)


def local_call(kernel, outs, ins, scratch=(), spaces=None, cost=None, mib=8):
    spaces = spaces or {}
    ins = [
        pltpu.with_memory_space_constraint(value, spaces[i])
        if spaces.get(i) in (pltpu.HBM, pltpu.VMEM)
        else value
        for i, value in enumerate(ins)
    ]
    return pl.pallas_call(
        kernel,
        out_shape=outs,
        in_specs=[pl.BlockSpec(memory_space=spaces.get(i, pltpu.VMEM)) for i in range(len(ins))],
        out_specs=jax.tree.map(lambda _: pl.BlockSpec(memory_space=pltpu.VMEM), outs),
        scratch_shapes=list(scratch),
        compiler_params=pltpu.CompilerParams(vmem_limit_bytes=mib << 20),
        cost_estimate=cost,
    )(*ins)


def swapped(value):
    return lax.ppermute(value, "core", [(0, 1), (1, 0)])


def exchanged(value, axes=SECTION):
    return lax.all_to_all(value, axes, 0, 0, tiled=True)


def per_device(
    arriving,
    entering,
    gain_attention,
    gain_key,
    decay_rate,
    state_in,
    gain_linear,
    gain_feed,
    gate_up,
    down_weight,
    prefix_keys,
    prefix_values,
    lengths,
):
    rows = arriving[0]
    parts = local_call(first_squares_kernel, shape_of(BLOCKS, HEAD, dtype=F32), (rows,))
    weights = local_call(
        prepare_kernel,
        shape_of(3 * UNITS, DIM),
        (gate_up[0], down_weight[0]),
        scratch=(pltpu.VMEM((UNITS, 2, DIM), BF16), pltpu.SemaphoreType.DMA((GROUPS + 1,))),
        spaces=dict.fromkeys(range(2), pltpu.HBM),
        cost=pl.CostEstimate(flops=0, bytes_accessed=8 << 20, transcendentals=0),
        mib=16,
    )
    prefix = jnp.concatenate([prefix_keys[0], prefix_values[0]], axis=0)
    prefix = jnp.transpose(prefix, (1, 0, 2))
    parts = exchanged(parts)
    prefix, parts = lax.optimization_barrier((prefix, parts))
    prefix = exchanged(prefix, ("x", "core"))
    prefix, sent_weights = lax.optimization_barrier((prefix, weights))
    far_weights = swapped(sent_weights)
    memory = state_in[0, 0]
    arrived = []
    for tick in range(TICKS):
        if tick:
            rows, parts = local_call(
                later_squares_kernel,
                (shape_of(TOK, HEAD), shape_of(BLOCKS, HEAD, dtype=F32)),
                (arrived[-1], entering[tick - 1]),
            )
            parts = exchanged(parts)
        outs = (
            shape_of(BLOCKS, HALF, HEAD),
            shape_of(TOK, HEAD),
            shape_of(HEAD, HEAD, dtype=F32),
            shape_of(2, TOK, HEAD),
        )
        ins = (decay_rate, parts, prefix, rows, memory)
        kernel = functools.partial(attention_kernel, tick)
        if tick == 0:
            spread, mixed, memory, turn, consts, prefix = local_call(
                kernel,
                (
                    *outs,
                    shape_of(8, SHARDS * ROWS, dtype=F32),
                    shape_of(SHARDS, 2 * ROWS, HEAD),
                ),
                (*ins, lengths, gain_attention, gain_key, gain_linear),
                scratch=(
                    pltpu.SMEM((1, SHARDS), jnp.int32),
                    pltpu.VMEM((3, 1, HEAD), F32),
                    pltpu.VMEM((BLOCKS, HEAD), F32),
                    pltpu.VMEM((TOK, HEAD), BF16),
                    pltpu.VMEM((HEAD, HEAD), F32),
                    pltpu.SemaphoreType.DMA((8,)),
                ),
                spaces={0: pltpu.SMEM, **dict.fromkeys(range(1, 9), pltpu.HBM)},
            )
        else:
            spread, mixed, memory, turn = local_call(
                kernel, outs, (*ins, turn, consts), spaces={0: pltpu.SMEM}
            )
        spread = exchanged(spread)
        down = local_call(
            feed_kernel,
            shape_of(BLOCKS, HALF, HEAD),
            (spread, gain_feed, weights, far_weights),
            scratch=(pltpu.VMEM((2, 2 * UNITS, HALF), F32),),
            mib=16,
        )
        down = exchanged(down)
        finished = local_call(finish_kernel, shape_of(TOK, HEAD), (down, mixed))
        size = lax.axis_size("section")
        arrived.append(
            lax.ppermute(finished, "section", [(i, (i + 1) % size) for i in range(size)])
        )
    return (jnp.stack(arrived)[:, None], memory[None, None])


def solution(mesh):
    shape = mesh.devices.shape
    split = jax.sharding.Mesh(
        mesh.devices.reshape(shape[0], shape[1] // 2, 2, shape[2]), ("section", "x", "core", "tp")
    )
    kv = ("x", "core")
    in_specs = (
        P("section", None, SECTION),
        P(None, None, SECTION),
        P("section", None),
        P("section", None),
        P("section", SECTION),
        P("section", SECTION, None, None),
        P("section", SECTION),
        P("section", None),
        P("section", SECTION, None, None),
        P("section", SECTION, None),
        P("section", kv, None, "tp"),
        P("section", kv, None, "tp"),
        P("section", None),
    )
    out_specs = (P(None, "section", None, SECTION), P("section", SECTION, None, None))
    return jax.shard_map(
        per_device, mesh=split, in_specs=in_specs, out_specs=out_specs, check_vma=False
    )
```

```python
import functools

import jax
import jax.numpy as jnp
from jax import lax
from jax.experimental import pallas as pl
from jax.experimental.pallas import tpu as pltpu
from jax.sharding import PartitionSpec as P

TICKS = 2
TOK = 128
HALF = 64
HEAD = 128
DIM = 4096
UNITS = 144
BLOCKS = 32
SHARDS = 8
ROWS = 64
TAIL = 16
GROUPS = 3
GROUP = UNITS // GROUPS
EPS = 1e-6
MASKED = -1e30
SECTION = ("x", "core", "tp")
F32 = jnp.float32
BF16 = jnp.bfloat16
HIGH = lax.Precision.HIGHEST


def dot(left, right, dims, precision=None):
    return lax.dot_general(
        left, right, ((dims[:1], dims[1:]), ((), ())), precision=precision, preferred_element_type=F32
    )


def block_place():
    return (lax.axis_index("x") * 2 + lax.axis_index("core")) * 4 + lax.axis_index("tp")


def write_square_sums(rows, parts_ref):
    squares = rows.astype(F32)
    squares = squares * squares
    sums = dot(jnp.ones((8, HEAD), F32), squares, (1, 1), HIGH)
    parts_ref[...] = jnp.concatenate([sums] * (BLOCKS // 8), axis=0)


def started(pairs, sems):
    copies = [pltpu.make_async_copy(*pair, sems.at[i]) for i, pair in enumerate(pairs)]
    for copy in copies:
        copy.start()
    return copies


def start_kernel(rows_hbm, keys_hbm, values_hbm, out_hbm, rows_ref, keys_ref, values_ref, out_ref, sems):
    copies = started(
        [(rows_hbm, rows_ref), (keys_hbm, keys_ref), (values_hbm, values_ref)], sems
    )
    copies[0].wait()
    squares = rows_ref[...].astype(F32)
    squares = squares * squares
    sums = dot(jnp.ones((TAIL, HEAD), F32), squares, (1, 1), HIGH)
    high = sums.astype(BF16).astype(F32)
    middle = (sums - high).astype(BF16).astype(F32)
    row = lax.broadcasted_iota(jnp.int32, (TAIL, HEAD), 0)
    tail = jnp.where(row == 2, sums - high - middle, 0.0)
    tail = jnp.where(row == 0, high, jnp.where(row == 1, middle, tail)).astype(BF16)
    for index, ref in enumerate((keys_ref, values_ref)):
        copies[1 + index].wait()
        by_head = jnp.swapaxes(ref[...], 0, 1)
        for shard in range(SHARDS):
            out_ref[shard, index * ROWS : (index + 1) * ROWS] = by_head[shard]
    for shard in range(SHARDS):
        out_ref[shard, 2 * ROWS :] = tail
    copy = pltpu.make_async_copy(out_ref, out_hbm, sems.at[3])
    copy.start()
    copy.wait()


def merge_kernel(
    decays_hbm,
    lengths_hbm,
    swapped_hbm,
    rows_hbm,
    memory_hbm,
    gain_hbm,
    key_gain_hbm,
    linear_gain_hbm,
    parts_ref,
    prefix_ref,
    rows_ref,
    memory_ref,
    consts_ref,
    lengths_ref,
    decays_ref,
    tails_ref,
    gains_ref,
    sems,
):
    place = pl.ds(pl.multiple_of(block_place() * HEAD, HEAD), HEAD)
    copies = started(
        [
            (swapped_hbm.at[:, pl.ds(2 * ROWS, TAIL)], tails_ref),
            (lengths_hbm, lengths_ref),
            (decays_hbm, decays_ref),
            (gain_hbm.at[:, place], gains_ref.at[0]),
            (key_gain_hbm.at[:, place], gains_ref.at[1]),
            (linear_gain_hbm, gains_ref.at[2]),
            (rows_hbm, rows_ref),
            (memory_hbm, memory_ref),
            (swapped_hbm.at[:, pl.ds(0, 2 * ROWS)], prefix_ref),
        ],
        sems,
    )
    copies[0].wait()
    tails = tails_ref[0].astype(F32)
    for shard in range(1, SHARDS):
        tails = tails + tails_ref[shard].astype(F32)
    sums = jnp.sum(tails, axis=0, keepdims=True) * (1.0 / 8)
    for target in range(4):
        parts_ref[target] = jnp.broadcast_to(sums, (8, HEAD))
    for copy in copies[1:]:
        copy.wait()
    slot = lax.broadcasted_iota(jnp.int32, (1, SHARDS * ROWS), 1)
    used = jnp.zeros((1, SHARDS * ROWS), jnp.int32)
    for shard in range(SHARDS):
        used = jnp.where(slot // ROWS == shard, lengths_ref[0, shard], used)
    consts_ref[0:1] = jnp.where(slot % ROWS < used, 0.0, MASKED)
    for index in range(3):
        consts_ref[1:2, index * HEAD : (index + 1) * HEAD] = gains_ref[index]
    consts_ref[1:2, 3 * HEAD :] = decays_ref[0:1]


def later_squares_kernel(passed_ref, entering_ref, rows_ref, parts_ref):
    rows = jnp.where(lax.axis_index("section") == 0, entering_ref[...], passed_ref[...])
    rows_ref[...] = rows
    write_square_sums(rows, parts_ref)


def attention_kernel(
    tick, parts_ref, consts_ref, prefix_ref, rows_ref, memory_ref, *refs
):
    scale = HEAD**-0.5
    if tick:
        past_ref, *refs = refs
    spread_ref, mixed_ref, new_memory_ref, turn_ref = refs
    barred = consts_ref[0:1]
    gain, key_gain, linear_gain, decay = [
        consts_ref[1:2, index * HEAD : (index + 1) * HEAD] for index in range(4)
    ]
    sums = dot(parts_ref[...], jnp.ones((BLOCKS, HEAD), F32), (0, 0), HIGH)
    rows = rows_ref[...].astype(F32)
    normed = rows * lax.rsqrt(sums * (1.0 / DIM) + EPS) * gain
    queries = normed.astype(BF16)
    keys = (normed * key_gain).astype(BF16)
    turn_ref[0] = keys
    turn_ref[1] = queries

    shape = (TOK, TOK)
    row = lax.broadcasted_iota(jnp.int32, shape, 0)
    column = lax.broadcasted_iota(jnp.int32, shape, 1)
    causal = column <= row
    own_scores = dot(queries, keys, (1, 1)) * scale
    age = jnp.where(causal, row - column, 0).astype(F32)
    weights = jnp.where(causal, own_scores * jnp.exp(-decay * age), 0.0).astype(BF16)
    row = row.astype(F32)
    memory = memory_ref[...]
    wide = queries.astype(F32)
    raw = dot(weights, queries, (1, 0)) + dot(wide, memory, (1, 0), HIGH) * jnp.exp(
        -decay * (row + 1.0)
    )
    tail = keys.astype(F32) * jnp.exp(-decay * (TOK - 1.0 - row))
    new_memory_ref[...] = memory * jnp.exp(-decay * TOK) + (
        dot(tail, wide, (0, 0), HIGH) * scale
    )
    spread = jnp.mean(raw * raw, axis=1, keepdims=True)
    linear = raw * lax.rsqrt(spread + EPS) * linear_gain

    prefix_keys = prefix_ref[:, :ROWS, :].reshape(SHARDS * ROWS, HEAD)
    prefix_values = prefix_ref[:, ROWS:, :].reshape(SHARDS * ROWS, HEAD)
    prefix_scores = dot(queries, prefix_keys, (1, 1)) * scale + barred
    groups = [
        (prefix_scores, prefix_values),
        (jnp.where(causal, own_scores, MASKED), queries),
    ]
    if tick:
        groups.append((dot(queries, past_ref[0], (1, 1)) * scale, past_ref[1]))
    top = functools.reduce(
        jnp.maximum, [jnp.max(scores, axis=1, keepdims=True) for scores, _ in groups]
    )
    total = 0.0
    weighted = 0.0
    for scores, values in groups:
        probabilities = jnp.exp(scores - top)
        total = total + jnp.sum(probabilities, axis=1, keepdims=True)
        weighted = weighted + dot(probabilities.astype(BF16), values, (1, 0))
    mixed = (rows + (linear + weighted / total)).astype(BF16)
    mixed_ref[...] = mixed
    for block in range(BLOCKS):
        half = block // 4 % 2
        spread_ref[block] = mixed[half * HALF : (half + 1) * HALF]


def feed_kernel(rows_ref, gain_ref, near_ref, far_ref, out_ref, wide_ref):
    step = 1024
    squares = jnp.zeros((HALF, HEAD), F32)
    sums = [0.0, 0.0]
    for first in range(0, DIM, step):
        place = slice(first, first + step)
        pieces = []
        for block in range(first // HEAD, (first + step) // HEAD):
            rows = rows_ref[block].astype(F32)
            squares = squares + rows * rows
            gain = gain_ref[:, block * HEAD : (block + 1) * HEAD]
            pieces.append((rows * gain).astype(BF16))
        feed = jnp.concatenate(pieces, axis=1)
        for side, ref in enumerate((near_ref, far_ref)):
            sums[side] = sums[side] + dot(ref[: 2 * UNITS, place], feed, (1, 1))
    mean = dot(jnp.ones((8, HEAD), F32), squares, (1, 1), HIGH)[:1] * (1.0 / DIM)
    factor = lax.rsqrt(mean + EPS)
    hidden = []
    for side in range(2):
        wide_ref[side] = sums[side]
        gate = wide_ref[side, pl.ds(0, UNITS, stride=2), :] * factor
        up = wide_ref[side, pl.ds(1, UNITS, stride=2), :] * factor
        hidden.append(jnp.transpose((gate / (1.0 + jnp.exp(-gate)) * up).astype(BF16)))
    for first in range(0, DIM, step):
        place = slice(first, first + step)
        down = dot(hidden[0], near_ref[2 * UNITS :, place], (1, 0)) + dot(
            hidden[1], far_ref[2 * UNITS :, place], (1, 0)
        )
        for block in range(step // HEAD):
            out_ref[first // HEAD + block] = down[:, block * HEAD : (block + 1) * HEAD].astype(BF16)


def prepare_kernel(decay_ref, gate_up_hbm, down_hbm, weights_ref, decays_ref, raw_ref, sems):
    decays_ref[...] = jnp.full((8, HEAD), decay_ref[0, 0], F32)
    pairs = []
    for group in range(GROUPS):
        span = pl.ds(group * GROUP, GROUP)
        pairs.append((gate_up_hbm.at[span], raw_ref.at[span]))
    pairs.append((down_hbm, weights_ref.at[pl.ds(2 * UNITS, UNITS)]))
    copies = started(pairs, sems)
    for group in range(GROUPS):
        copies[group].wait()

        @pl.loop(0, GROUP // 16)
        def _(part):
            raw = raw_ref[pl.ds(group * GROUP + part * 16, 16)]
            target = pl.ds(pl.multiple_of(2 * group * GROUP + part * 32, 32), 32)
            weights_ref[target] = raw.reshape(32, DIM)

    copies[GROUPS].wait()


def finish_kernel(parts_ref, mixed_ref, out_ref):
    for half in range(2):
        place = slice(half * HALF, (half + 1) * HALF)
        total = mixed_ref[place].astype(F32)
        for block in range(BLOCKS):
            if block // 4 % 2 == half:
                total = total + parts_ref[block].astype(F32)
        out_ref[place] = total.astype(BF16)


def shape_of(*shape, dtype=BF16):
    return jax.ShapeDtypeStruct(shape, dtype)


def local_call(kernel, outs, ins, scratch=(), spaces=None, out_space=pltpu.VMEM, cost=None, mib=8):
    spaces = spaces or {}
    ins = [
        pltpu.with_memory_space_constraint(value, spaces[i])
        if spaces.get(i) in (pltpu.HBM, pltpu.VMEM)
        else value
        for i, value in enumerate(ins)
    ]
    return pl.pallas_call(
        kernel,
        out_shape=outs,
        in_specs=[pl.BlockSpec(memory_space=spaces.get(i, pltpu.VMEM)) for i in range(len(ins))],
        out_specs=jax.tree.map(lambda _: pl.BlockSpec(memory_space=out_space), outs),
        scratch_shapes=list(scratch),
        compiler_params=pltpu.CompilerParams(vmem_limit_bytes=mib << 20),
        cost_estimate=cost,
    )(*ins)


def swapped(value):
    return lax.ppermute(value, "core", [(0, 1), (1, 0)])


def exchanged(value, axes=SECTION):
    return lax.all_to_all(value, axes, 0, 0, tiled=True)


def per_device(
    arriving,
    entering,
    gain_attention,
    gain_key,
    decay_rate,
    state_in,
    gain_linear,
    gain_feed,
    gate_up,
    down_weight,
    prefix_keys,
    prefix_values,
    lengths,
):
    rows = arriving[0]
    sent = local_call(
        start_kernel,
        shape_of(SHARDS, 2 * ROWS + TAIL, HEAD),
        (rows, prefix_keys[0], prefix_values[0]),
        scratch=(
            pltpu.VMEM((TOK, HEAD), BF16),
            pltpu.VMEM((ROWS, SHARDS, HEAD), BF16),
            pltpu.VMEM((ROWS, SHARDS, HEAD), BF16),
            pltpu.VMEM((SHARDS, 2 * ROWS + TAIL, HEAD), BF16),
            pltpu.SemaphoreType.DMA((4,)),
        ),
        spaces=dict.fromkeys(range(3), pltpu.HBM),
        out_space=pltpu.HBM,
    )
    sent = exchanged(sent, ("x", "core"))
    weights, decays = local_call(
        prepare_kernel,
        (shape_of(3 * UNITS, DIM), shape_of(8, HEAD, dtype=F32)),
        (decay_rate, gate_up[0], down_weight[0]),
        scratch=(pltpu.VMEM((UNITS, 2, DIM), BF16), pltpu.SemaphoreType.DMA((GROUPS + 1,))),
        spaces={0: pltpu.SMEM, 1: pltpu.HBM, 2: pltpu.HBM},
        cost=pl.CostEstimate(flops=0, bytes_accessed=8 << 20, transcendentals=0),
        mib=16,
    )
    parts, prefix, rows, memory, consts = local_call(
        merge_kernel,
        (
            shape_of(4, 8, HEAD, dtype=F32),
            shape_of(SHARDS, 2 * ROWS, HEAD),
            shape_of(TOK, HEAD),
            shape_of(HEAD, HEAD, dtype=F32),
            shape_of(8, SHARDS * ROWS, dtype=F32),
        ),
        (
            decays,
            lengths,
            sent,
            rows,
            state_in[0, 0],
            gain_attention,
            gain_key,
            gain_linear,
        ),
        scratch=(
            pltpu.SMEM((1, SHARDS), jnp.int32),
            pltpu.VMEM((8, HEAD), F32),
            pltpu.VMEM((SHARDS, TAIL, HEAD), BF16),
            pltpu.VMEM((3, 1, HEAD), F32),
            pltpu.SemaphoreType.DMA((9,)),
        ),
        spaces=dict.fromkeys(range(8), pltpu.HBM),
    )
    parts, sent_weights = lax.optimization_barrier((parts, weights))
    far_weights = swapped(sent_weights)
    parts = exchanged(parts, "tp").reshape(BLOCKS, HEAD)
    size = lax.axis_size("section")
    onward = [(i, (i + 1) % size) for i in range(size)]
    past = ()
    arrived = []
    for tick in range(TICKS):
        if tick:
            rows, parts = local_call(
                later_squares_kernel,
                (shape_of(TOK, HEAD), shape_of(BLOCKS, HEAD, dtype=F32)),
                (passed, entering[tick - 1]),
            )
            parts = exchanged(parts)
        spread, mixed, memory, turn = local_call(
            functools.partial(attention_kernel, tick),
            (
                shape_of(BLOCKS, HALF, HEAD),
                shape_of(TOK, HEAD),
                shape_of(HEAD, HEAD, dtype=F32),
                shape_of(2, TOK, HEAD),
            ),
            (parts, consts, prefix, rows, memory, *past),
        )
        past = (turn,)
        spread = exchanged(spread)
        down = local_call(
            feed_kernel,
            shape_of(BLOCKS, HALF, HEAD),
            (spread, gain_feed, weights, far_weights),
            scratch=(pltpu.VMEM((2, 2 * UNITS, HALF), F32),),
            mib=16,
        )
        down = exchanged(down)
        finished = local_call(finish_kernel, shape_of(TOK, HEAD), (down, mixed))
        passed = lax.ppermute(finished, "section", onward)
        arrived.append(passed)
    return (jnp.stack(arrived)[:, None], memory[None, None])


def solution(mesh):
    shape = mesh.devices.shape
    split = jax.sharding.Mesh(
        mesh.devices.reshape(shape[0], shape[1] // 2, 2, shape[2]), ("section", "x", "core", "tp")
    )
    kv = ("x", "core")
    in_specs = (
        P("section", None, SECTION),
        P(None, None, SECTION),
        P("section", None),
        P("section", None),
        P("section", SECTION),
        P("section", SECTION, None, None),
        P("section", SECTION),
        P("section", None),
        P("section", SECTION, None, None),
        P("section", SECTION, None),
        P("section", kv, None, "tp"),
        P("section", kv, None, "tp"),
        P("section", None),
    )
    out_specs = (P(None, "section", None, SECTION), P("section", SECTION, None, None))
    return jax.shard_map(
        per_device, mesh=split, in_specs=in_specs, out_specs=out_specs, check_vma=False
    )
```

```python
import functools

import jax
import jax.numpy as jnp
from jax import lax
from jax.experimental import pallas as pl
from jax.experimental.pallas import tpu as pltpu
from jax.sharding import PartitionSpec as P

TICKS = 2
TOK = 128
HALF = 64
HEAD = 128
DIM = 4096
UNITS = 144
BLOCKS = 32
SHARDS = 8
ROWS = 64
TAIL = 16
GROUPS = 3
GROUP = UNITS // GROUPS
EPS = 1e-6
MASKED = -1e30
SECTION = ("x", "core", "tp")
F32 = jnp.float32
BF16 = jnp.bfloat16
HIGH = lax.Precision.HIGHEST


def dot(left, right, dims, precision=None):
    return lax.dot_general(
        left, right, ((dims[:1], dims[1:]), ((), ())), precision=precision, preferred_element_type=F32
    )


def block_place():
    return (lax.axis_index("x") * 2 + lax.axis_index("core")) * 4 + lax.axis_index("tp")


def write_square_sums(rows, parts_ref):
    squares = rows.astype(F32)
    squares = squares * squares
    sums = dot(jnp.ones((8, HEAD), F32), squares, (1, 1), HIGH)
    parts_ref[...] = jnp.concatenate([sums] * (BLOCKS // 8), axis=0)


def started(pairs, sems):
    copies = [pltpu.make_async_copy(*pair, sems.at[i]) for i, pair in enumerate(pairs)]
    for copy in copies:
        copy.start()
    return copies


def start_kernel(rows_hbm, keys_hbm, values_hbm, out_hbm, rows_ref, keys_ref, values_ref, out_ref, sems):
    copies = started(
        [(rows_hbm, rows_ref), (keys_hbm, keys_ref), (values_hbm, values_ref)], sems
    )
    copies[0].wait()
    squares = rows_ref[...].astype(F32)
    squares = squares * squares
    sums = dot(jnp.ones((TAIL, HEAD), F32), squares, (1, 1), HIGH)
    high = sums.astype(BF16).astype(F32)
    middle = (sums - high).astype(BF16).astype(F32)
    row = lax.broadcasted_iota(jnp.int32, (TAIL, HEAD), 0)
    tail = jnp.where(row == 2, sums - high - middle, 0.0)
    tail = jnp.where(row == 0, high, jnp.where(row == 1, middle, tail)).astype(BF16)
    for index, ref in enumerate((keys_ref, values_ref)):
        copies[1 + index].wait()
        by_head = jnp.swapaxes(ref[...], 0, 1)
        span = pl.ds(index * ROWS, ROWS)
        for shard in range(SHARDS):
            out_ref[shard, span] = by_head[shard]
            if index:
                out_ref[shard, 2 * ROWS :] = tail
        span = pl.ds(index * ROWS, ROWS + index * TAIL)
        copies.append(
            pltpu.make_async_copy(out_ref.at[:, span], out_hbm.at[:, span], sems.at[3 + index])
        )
        copies[-1].start()
    for copy in copies[3:]:
        copy.wait()


def merge_kernel(
    decays_hbm,
    lengths_hbm,
    swapped_hbm,
    rows_hbm,
    memory_hbm,
    gain_hbm,
    key_gain_hbm,
    linear_gain_hbm,
    parts_ref,
    prefix_ref,
    rows_ref,
    memory_ref,
    consts_ref,
    lengths_ref,
    decays_ref,
    tails_ref,
    gains_ref,
    sems,
):
    place = pl.ds(pl.multiple_of(block_place() * HEAD, HEAD), HEAD)
    copies = started(
        [
            (swapped_hbm.at[:, pl.ds(2 * ROWS, TAIL)], tails_ref),
            (lengths_hbm, lengths_ref),
            (decays_hbm, decays_ref),
            (gain_hbm.at[:, place], gains_ref.at[0]),
            (key_gain_hbm.at[:, place], gains_ref.at[1]),
            (linear_gain_hbm, gains_ref.at[2]),
            (rows_hbm, rows_ref),
            (memory_hbm, memory_ref),
            (swapped_hbm.at[:, pl.ds(0, 2 * ROWS)], prefix_ref),
        ],
        sems,
    )
    copies[0].wait()
    tails = tails_ref[0].astype(F32)
    for shard in range(1, SHARDS):
        tails = tails + tails_ref[shard].astype(F32)
    sums = jnp.sum(tails, axis=0, keepdims=True) * (1.0 / 8)
    for target in range(4):
        parts_ref[target] = jnp.broadcast_to(sums, (8, HEAD))
    for copy in copies[1:]:
        copy.wait()
    slot = lax.broadcasted_iota(jnp.int32, (1, SHARDS * ROWS), 1)
    used = jnp.zeros((1, SHARDS * ROWS), jnp.int32)
    for shard in range(SHARDS):
        used = jnp.where(slot // ROWS == shard, lengths_ref[0, shard], used)
    consts_ref[0:1] = jnp.where(slot % ROWS < used, 0.0, MASKED)
    for index in range(3):
        consts_ref[1:2, index * HEAD : (index + 1) * HEAD] = gains_ref[index]
    consts_ref[1:2, 3 * HEAD :] = decays_ref[0:1]


def later_squares_kernel(passed_ref, entering_ref, rows_ref, parts_ref):
    rows = jnp.where(lax.axis_index("section") == 0, entering_ref[...], passed_ref[...])
    rows_ref[...] = rows
    write_square_sums(rows, parts_ref)


def memory_kernel(consts_ref, memory_ref, turn_ref, out_ref):
    decay = consts_ref[1:2, 3 * HEAD :]
    row = lax.broadcasted_iota(jnp.int32, (TOK, HEAD), 0).astype(F32)
    tail = turn_ref[0].astype(F32) * jnp.exp(-decay * (TOK - 1.0 - row))
    update = dot(tail, turn_ref[1].astype(F32), (0, 0), HIGH) * HEAD**-0.5
    out_ref[...] = memory_ref[...] * jnp.exp(-decay * TOK) + update


def attention_kernel(
    tick, parts_ref, consts_ref, prefix_ref, rows_ref, memory_ref, *refs
):
    scale = HEAD**-0.5
    if tick:
        past_ref, *refs = refs
    spread_ref, mixed_ref, turn_ref = refs[:3]
    barred = consts_ref[0:1]
    gain, key_gain, linear_gain, decay = [
        consts_ref[1:2, index * HEAD : (index + 1) * HEAD] for index in range(4)
    ]
    sums = dot(parts_ref[...], jnp.ones((BLOCKS, HEAD), F32), (0, 0), HIGH)
    rows = rows_ref[...].astype(F32)
    normed = rows * lax.rsqrt(sums * (1.0 / DIM) + EPS) * gain
    queries = normed.astype(BF16)
    keys = (normed * key_gain).astype(BF16)
    turn_ref[0] = keys
    turn_ref[1] = queries
    if tick == 0:
        memory_kernel(consts_ref, memory_ref, turn_ref, refs[3])

    shape = (TOK, TOK)
    row = lax.broadcasted_iota(jnp.int32, shape, 0)
    column = lax.broadcasted_iota(jnp.int32, shape, 1)
    causal = column <= row
    own_scores = dot(queries, keys, (1, 1)) * scale
    age = jnp.where(causal, row - column, 0).astype(F32)
    weights = jnp.where(causal, own_scores * jnp.exp(-decay * age), 0.0).astype(BF16)
    row = row.astype(F32)
    memory = memory_ref[...]
    wide = queries.astype(F32)
    raw = dot(weights, queries, (1, 0)) + dot(wide, memory, (1, 0), HIGH) * jnp.exp(
        -decay * (row + 1.0)
    )
    spread = jnp.mean(raw * raw, axis=1, keepdims=True)
    linear = raw * lax.rsqrt(spread + EPS) * linear_gain

    prefix_keys = prefix_ref[:, :ROWS, :].reshape(SHARDS * ROWS, HEAD)
    prefix_values = prefix_ref[:, ROWS:, :].reshape(SHARDS * ROWS, HEAD)
    prefix_scores = dot(queries, prefix_keys, (1, 1)) * scale + barred
    groups = [
        (prefix_scores, prefix_values),
        (jnp.where(causal, own_scores, MASKED), queries),
    ]
    if tick:
        groups.append((dot(queries, past_ref[0], (1, 1)) * scale, past_ref[1]))
    top = functools.reduce(
        jnp.maximum, [jnp.max(scores, axis=1, keepdims=True) for scores, _ in groups]
    )
    total = 0.0
    weighted = 0.0
    for scores, values in groups:
        probabilities = jnp.exp(scores - top)
        total = total + jnp.sum(probabilities, axis=1, keepdims=True)
        weighted = weighted + dot(probabilities.astype(BF16), values, (1, 0))
    mixed = (rows + (linear + weighted / total)).astype(BF16)
    mixed_ref[...] = mixed
    for block in range(BLOCKS):
        half = block // 4 % 2
        spread_ref[block] = mixed[half * HALF : (half + 1) * HALF]


def feed_kernel(rows_ref, gain_ref, near_ref, far_ref, out_ref, wide_ref):
    step = 1024
    squares = jnp.zeros((HALF, HEAD), F32)
    sums = [0.0, 0.0]
    for first in range(0, DIM, step):
        place = slice(first, first + step)
        pieces = []
        for block in range(first // HEAD, (first + step) // HEAD):
            rows = rows_ref[block].astype(F32)
            squares = squares + rows * rows
            gain = gain_ref[:, block * HEAD : (block + 1) * HEAD]
            pieces.append((rows * gain).astype(BF16))
        feed = jnp.concatenate(pieces, axis=1)
        for side, ref in enumerate((near_ref, far_ref)):
            sums[side] = sums[side] + dot(ref[: 2 * UNITS, place], feed, (1, 1))
    mean = dot(jnp.ones((8, HEAD), F32), squares, (1, 1), HIGH)[:1] * (1.0 / DIM)
    factor = lax.rsqrt(mean + EPS)
    hidden = []
    for side in range(2):
        wide_ref[side] = sums[side]
        gate = wide_ref[side, pl.ds(0, UNITS, stride=2), :] * factor
        up = wide_ref[side, pl.ds(1, UNITS, stride=2), :] * factor
        hidden.append(jnp.transpose((gate / (1.0 + jnp.exp(-gate)) * up).astype(BF16)))
    for first in range(0, DIM, step):
        place = slice(first, first + step)
        down = dot(hidden[0], near_ref[2 * UNITS :, place], (1, 0)) + dot(
            hidden[1], far_ref[2 * UNITS :, place], (1, 0)
        )
        for block in range(step // HEAD):
            out_ref[first // HEAD + block] = down[:, block * HEAD : (block + 1) * HEAD].astype(BF16)


def prepare_kernel(decay_ref, gate_up_hbm, down_hbm, weights_ref, decays_ref, raw_ref, sems):
    decays_ref[...] = jnp.full((8, HEAD), decay_ref[0, 0], F32)
    pairs = []
    for group in range(GROUPS):
        span = pl.ds(group * GROUP, GROUP)
        pairs.append((gate_up_hbm.at[span], raw_ref.at[span]))
    pairs.append((down_hbm, weights_ref.at[pl.ds(2 * UNITS, UNITS)]))
    copies = started(pairs, sems)
    for group in range(GROUPS):
        copies[group].wait()

        @pl.loop(0, GROUP // 16)
        def _(part):
            raw = raw_ref[pl.ds(group * GROUP + part * 16, 16)]
            target = pl.ds(pl.multiple_of(2 * group * GROUP + part * 32, 32), 32)
            weights_ref[target] = raw.reshape(32, DIM)

    copies[GROUPS].wait()


def finish_kernel(parts_ref, mixed_ref, out_ref):
    for half in range(2):
        place = slice(half * HALF, (half + 1) * HALF)
        total = mixed_ref[place].astype(F32)
        for block in range(BLOCKS):
            if block // 4 % 2 == half:
                total = total + parts_ref[block].astype(F32)
        out_ref[place] = total.astype(BF16)


def shape_of(*shape, dtype=BF16):
    return jax.ShapeDtypeStruct(shape, dtype)


def local_call(kernel, outs, ins, scratch=(), spaces=None, out_space=pltpu.VMEM, cost=None, mib=8):
    spaces = spaces or {}
    ins = [
        pltpu.with_memory_space_constraint(value, spaces[i])
        if spaces.get(i) in (pltpu.HBM, pltpu.VMEM)
        else value
        for i, value in enumerate(ins)
    ]
    return pl.pallas_call(
        kernel,
        out_shape=outs,
        in_specs=[pl.BlockSpec(memory_space=spaces.get(i, pltpu.VMEM)) for i in range(len(ins))],
        out_specs=jax.tree.map(lambda _: pl.BlockSpec(memory_space=out_space), outs),
        scratch_shapes=list(scratch),
        compiler_params=pltpu.CompilerParams(vmem_limit_bytes=mib << 20),
        cost_estimate=cost,
    )(*ins)


def swapped(value):
    return lax.ppermute(value, "core", [(0, 1), (1, 0)])


def exchanged(value, axes=SECTION):
    return lax.all_to_all(value, axes, 0, 0, tiled=True)


def per_device(
    arriving,
    entering,
    gain_attention,
    gain_key,
    decay_rate,
    state_in,
    gain_linear,
    gain_feed,
    gate_up,
    down_weight,
    prefix_keys,
    prefix_values,
    lengths,
):
    rows = arriving[0]
    sent = local_call(
        start_kernel,
        shape_of(SHARDS, 2 * ROWS + TAIL, HEAD),
        (rows, prefix_keys[0], prefix_values[0]),
        scratch=(
            pltpu.VMEM((TOK, HEAD), BF16),
            pltpu.VMEM((ROWS, SHARDS, HEAD), BF16),
            pltpu.VMEM((ROWS, SHARDS, HEAD), BF16),
            pltpu.VMEM((SHARDS, 2 * ROWS + TAIL, HEAD), BF16),
            pltpu.SemaphoreType.DMA((5,)),
        ),
        spaces=dict.fromkeys(range(3), pltpu.HBM),
        out_space=pltpu.HBM,
    )
    sent = exchanged(sent, ("x", "core"))
    weights, decays = local_call(
        prepare_kernel,
        (shape_of(3 * UNITS, DIM), shape_of(8, HEAD, dtype=F32)),
        (decay_rate, gate_up[0], down_weight[0]),
        scratch=(pltpu.VMEM((UNITS, 2, DIM), BF16), pltpu.SemaphoreType.DMA((GROUPS + 1,))),
        spaces={0: pltpu.SMEM, 1: pltpu.HBM, 2: pltpu.HBM},
        cost=pl.CostEstimate(flops=0, bytes_accessed=8 << 20, transcendentals=0),
        mib=16,
    )
    parts, prefix, rows, memory, consts = local_call(
        merge_kernel,
        (
            shape_of(4, 8, HEAD, dtype=F32),
            shape_of(SHARDS, 2 * ROWS, HEAD),
            shape_of(TOK, HEAD),
            shape_of(HEAD, HEAD, dtype=F32),
            shape_of(8, SHARDS * ROWS, dtype=F32),
        ),
        (
            decays,
            lengths,
            sent,
            rows,
            state_in[0, 0],
            gain_attention,
            gain_key,
            gain_linear,
        ),
        scratch=(
            pltpu.SMEM((1, SHARDS), jnp.int32),
            pltpu.VMEM((8, HEAD), F32),
            pltpu.VMEM((SHARDS, TAIL, HEAD), BF16),
            pltpu.VMEM((3, 1, HEAD), F32),
            pltpu.SemaphoreType.DMA((9,)),
        ),
        spaces=dict.fromkeys(range(8), pltpu.HBM),
    )
    parts, sent_weights = lax.optimization_barrier((parts, weights))
    far_weights = swapped(sent_weights)
    parts = exchanged(parts, "tp").reshape(BLOCKS, HEAD)
    size = lax.axis_size("section")
    onward = [(i, (i + 1) % size) for i in range(size)]
    past = ()
    arrived = []
    for tick in range(TICKS):
        if tick:
            rows, parts = local_call(
                later_squares_kernel,
                (shape_of(TOK, HEAD), shape_of(BLOCKS, HEAD, dtype=F32)),
                (passed, entering[tick - 1]),
            )
            parts = exchanged(parts)
        outs = (shape_of(BLOCKS, HALF, HEAD), shape_of(TOK, HEAD), shape_of(2, TOK, HEAD))
        state = shape_of(HEAD, HEAD, dtype=F32)
        kernel = functools.partial(attention_kernel, tick)
        ins = (parts, consts, prefix, rows, memory, *past)
        if tick == 0:
            spread, mixed, turn, memory = local_call(kernel, (*outs, state), ins)
        else:
            spread, mixed, turn = local_call(kernel, outs, ins)
            memory = local_call(memory_kernel, state, (consts, memory, turn))
        past = (turn,)
        spread = exchanged(spread)
        down = local_call(
            feed_kernel,
            shape_of(BLOCKS, HALF, HEAD),
            (spread, gain_feed, weights, far_weights),
            scratch=(pltpu.VMEM((2, 2 * UNITS, HALF), F32),),
            mib=16,
        )
        down = exchanged(down)
        finished = local_call(finish_kernel, shape_of(TOK, HEAD), (down, mixed))
        passed = lax.ppermute(finished, "section", onward)
        arrived.append(passed)
    return (jnp.stack(arrived)[:, None], memory[None, None])


def solution(mesh):
    shape = mesh.devices.shape
    split = jax.sharding.Mesh(
        mesh.devices.reshape(shape[0], shape[1] // 2, 2, shape[2]), ("section", "x", "core", "tp")
    )
    kv = ("x", "core")
    in_specs = (
        P("section", None, SECTION),
        P(None, None, SECTION),
        P("section", None),
        P("section", None),
        P("section", SECTION),
        P("section", SECTION, None, None),
        P("section", SECTION),
        P("section", None),
        P("section", SECTION, None, None),
        P("section", SECTION, None),
        P("section", kv, None, "tp"),
        P("section", kv, None, "tp"),
        P("section", None),
    )
    out_specs = (P(None, "section", None, SECTION), P("section", SECTION, None, None))
    return jax.shard_map(
        per_device, mesh=split, in_specs=in_specs, out_specs=out_specs, check_vma=False
    )
```

```python
import functools

import jax
import jax.numpy as jnp
from jax import lax
from jax.experimental import pallas as pl
from jax.experimental.pallas import tpu as pltpu
from jax.sharding import PartitionSpec as P

TICKS = 2
TOK = 128
HALF = 64
HEAD = 128
DIM = 4096
UNITS = 144
BLOCKS = 32
SHARDS = 8
ROWS = 64
TAIL = 16
GROUPS = 3
GROUP = UNITS // GROUPS
EPS = 1e-6
MASKED = -1e30
SECTION = ("x", "core", "tp")
PEERS = ("core", "x", "tp")
F32 = jnp.float32
BF16 = jnp.bfloat16
HIGH = lax.Precision.HIGHEST


def dot(left, right, dims, precision=None):
    return lax.dot_general(
        left, right, ((dims[:1], dims[1:]), ((), ())), precision=precision, preferred_element_type=F32
    )


def peer(block):
    return block // 4 % 2 * 16 + block // 8 * 4 + block % 4


def block_place():
    return (lax.axis_index("x") * 2 + lax.axis_index("core")) * 4 + lax.axis_index("tp")


def write_square_sums(rows, parts_ref):
    squares = rows.astype(F32)
    squares = squares * squares
    sums = dot(jnp.ones((8, HEAD), F32), squares, (1, 1), HIGH)
    parts_ref[...] = jnp.concatenate([sums] * (BLOCKS // 8), axis=0)


def started(pairs, sems):
    copies = [pltpu.make_async_copy(*pair, sems.at[i]) for i, pair in enumerate(pairs)]
    for copy in copies:
        copy.start()
    return copies


def start_kernel(rows_hbm, keys_hbm, values_hbm, out_hbm, rows_ref, keys_ref, values_ref, out_ref, sems):
    copies = started(
        [(rows_hbm, rows_ref), (keys_hbm, keys_ref), (values_hbm, values_ref)], sems
    )
    copies[0].wait()
    squares = rows_ref[...].astype(F32)
    squares = squares * squares
    sums = dot(jnp.ones((TAIL, HEAD), F32), squares, (1, 1), HIGH)
    high = sums.astype(BF16).astype(F32)
    middle = (sums - high).astype(BF16).astype(F32)
    row = lax.broadcasted_iota(jnp.int32, (TAIL, HEAD), 0)
    tail = jnp.where(row == 2, sums - high - middle, 0.0)
    tail = jnp.where(row == 0, high, jnp.where(row == 1, middle, tail)).astype(BF16)
    for index, ref in enumerate((keys_ref, values_ref)):
        copies[1 + index].wait()
        by_head = jnp.swapaxes(ref[...], 0, 1)
        span = pl.ds(index * ROWS, ROWS)
        for shard in range(SHARDS):
            out_ref[shard, span] = by_head[shard]
            if index:
                out_ref[shard, 2 * ROWS :] = tail
        span = pl.ds(index * ROWS, ROWS + index * TAIL)
        copies.append(
            pltpu.make_async_copy(out_ref.at[:, span], out_hbm.at[:, span], sems.at[3 + index])
        )
        copies[-1].start()
    for copy in copies[3:]:
        copy.wait()


def merge_kernel(
    decays_hbm,
    lengths_hbm,
    swapped_hbm,
    rows_hbm,
    memory_hbm,
    gain_hbm,
    key_gain_hbm,
    linear_gain_hbm,
    parts_ref,
    prefix_ref,
    rows_ref,
    memory_ref,
    consts_ref,
    lengths_ref,
    decays_ref,
    tails_ref,
    gains_ref,
    sems,
):
    place = pl.ds(pl.multiple_of(block_place() * HEAD, HEAD), HEAD)
    copies = started(
        [
            (swapped_hbm.at[:, pl.ds(2 * ROWS, TAIL)], tails_ref),
            (lengths_hbm, lengths_ref),
            (decays_hbm, decays_ref),
            (gain_hbm.at[:, place], gains_ref.at[0]),
            (key_gain_hbm.at[:, place], gains_ref.at[1]),
            (linear_gain_hbm, gains_ref.at[2]),
            (rows_hbm, rows_ref),
            (memory_hbm, memory_ref),
            (swapped_hbm.at[:, pl.ds(0, 2 * ROWS)], prefix_ref),
        ],
        sems,
    )
    copies[0].wait()
    tails = tails_ref[0].astype(F32)
    for shard in range(1, SHARDS):
        tails = tails + tails_ref[shard].astype(F32)
    sums = jnp.sum(tails, axis=0, keepdims=True) * (1.0 / 8)
    for target in range(4):
        parts_ref[target] = jnp.broadcast_to(sums, (8, HEAD))
    for copy in copies[1:]:
        copy.wait()
    slot = lax.broadcasted_iota(jnp.int32, (1, SHARDS * ROWS), 1)
    used = jnp.zeros((1, SHARDS * ROWS), jnp.int32)
    for shard in range(SHARDS):
        used = jnp.where(slot // ROWS == shard, lengths_ref[0, shard], used)
    consts_ref[0:1] = jnp.where(slot % ROWS < used, 0.0, MASKED)
    for index in range(3):
        consts_ref[1:2, index * HEAD : (index + 1) * HEAD] = gains_ref[index]
    consts_ref[1:2, 3 * HEAD :] = decays_ref[0:1]


def later_squares_kernel(passed_ref, entering_ref, rows_ref, parts_ref):
    rows = jnp.where(lax.axis_index("section") == 0, entering_ref[...], passed_ref[...])
    rows_ref[...] = rows
    write_square_sums(rows, parts_ref)


def memory_kernel(consts_ref, memory_ref, turn_ref, out_ref):
    decay = consts_ref[1:2, 3 * HEAD :]
    row = lax.broadcasted_iota(jnp.int32, (TOK, HEAD), 0).astype(F32)
    tail = turn_ref[0].astype(F32) * jnp.exp(-decay * (TOK - 1.0 - row))
    update = dot(tail, turn_ref[1].astype(F32), (0, 0), HIGH) * HEAD**-0.5
    out_ref[...] = memory_ref[...] * jnp.exp(-decay * TOK) + update


def attention_kernel(
    tick, parts_ref, consts_ref, prefix_ref, rows_ref, memory_ref, *refs
):
    scale = HEAD**-0.5
    if tick:
        past_ref, *refs = refs
    spread_ref, mixed_ref, turn_ref = refs[:3]
    barred = consts_ref[0:1]
    gain, key_gain, linear_gain, decay = [
        consts_ref[1:2, index * HEAD : (index + 1) * HEAD] for index in range(4)
    ]
    sums = dot(parts_ref[...], jnp.ones((BLOCKS, HEAD), F32), (0, 0), HIGH)
    rows = rows_ref[...].astype(F32)
    normed = rows * lax.rsqrt(sums * (1.0 / DIM) + EPS) * gain
    queries = normed.astype(BF16)
    keys = (normed * key_gain).astype(BF16)
    turn_ref[0] = keys
    turn_ref[1] = queries
    if tick == 0:
        memory_kernel(consts_ref, memory_ref, turn_ref, refs[3])

    shape = (TOK, TOK)
    row = lax.broadcasted_iota(jnp.int32, shape, 0)
    column = lax.broadcasted_iota(jnp.int32, shape, 1)
    causal = column <= row
    own_scores = dot(queries, keys, (1, 1)) * scale
    age = jnp.where(causal, row - column, 0).astype(F32)
    weights = jnp.where(causal, own_scores * jnp.exp(-decay * age), 0.0).astype(BF16)
    row = row.astype(F32)
    memory = memory_ref[...]
    wide = queries.astype(F32)
    raw = dot(weights, queries, (1, 0)) + dot(wide, memory, (1, 0), HIGH) * jnp.exp(
        -decay * (row + 1.0)
    )
    spread = jnp.mean(raw * raw, axis=1, keepdims=True)
    linear = raw * lax.rsqrt(spread + EPS) * linear_gain

    prefix_keys = prefix_ref[:, :ROWS, :].reshape(SHARDS * ROWS, HEAD)
    prefix_values = prefix_ref[:, ROWS:, :].reshape(SHARDS * ROWS, HEAD)
    prefix_scores = dot(queries, prefix_keys, (1, 1)) * scale + barred
    groups = [
        (prefix_scores, prefix_values),
        (jnp.where(causal, own_scores, MASKED), queries),
    ]
    if tick:
        groups.append((dot(queries, past_ref[0], (1, 1)) * scale, past_ref[1]))
    top = functools.reduce(
        jnp.maximum, [jnp.max(scores, axis=1, keepdims=True) for scores, _ in groups]
    )
    total = 0.0
    weighted = 0.0
    for scores, values in groups:
        probabilities = jnp.exp(scores - top)
        total = total + jnp.sum(probabilities, axis=1, keepdims=True)
        weighted = weighted + dot(probabilities.astype(BF16), values, (1, 0))
    mixed = (rows + (linear + weighted / total)).astype(BF16)
    mixed_ref[...] = mixed
    for block in range(BLOCKS):
        half = block // 4 % 2
        spread_ref[peer(block)] = mixed[half * HALF : (half + 1) * HALF]


def feed_kernel(rows_ref, gain_ref, near_ref, far_ref, out_ref, wide_ref):
    step = 1024
    squares = jnp.zeros((HALF, HEAD), F32)
    sums = [0.0, 0.0]
    for first in range(0, DIM, step):
        place = slice(first, first + step)
        pieces = []
        for block in range(first // HEAD, (first + step) // HEAD):
            rows = rows_ref[peer(block)].astype(F32)
            squares = squares + rows * rows
            gain = gain_ref[:, block * HEAD : (block + 1) * HEAD]
            pieces.append((rows * gain).astype(BF16))
        feed = jnp.concatenate(pieces, axis=1)
        for side, ref in enumerate((near_ref, far_ref)):
            sums[side] = sums[side] + dot(ref[: 2 * UNITS, place], feed, (1, 1))
    mean = dot(jnp.ones((8, HEAD), F32), squares, (1, 1), HIGH)[:1] * (1.0 / DIM)
    factor = lax.rsqrt(mean + EPS)
    hidden = []
    for side in range(2):
        wide_ref[side] = sums[side]
        gate = wide_ref[side, pl.ds(0, UNITS, stride=2), :] * factor
        up = wide_ref[side, pl.ds(1, UNITS, stride=2), :] * factor
        hidden.append(jnp.transpose((gate / (1.0 + jnp.exp(-gate)) * up).astype(BF16)))
    for first in range(0, DIM, step):
        place = slice(first, first + step)
        down = dot(hidden[0], near_ref[2 * UNITS :, place], (1, 0)) + dot(
            hidden[1], far_ref[2 * UNITS :, place], (1, 0)
        )
        for block in range(step // HEAD):
            out_ref[peer(first // HEAD + block)] = down[:, block * HEAD : (block + 1) * HEAD].astype(BF16)


def prepare_kernel(decay_ref, gate_up_hbm, down_hbm, weights_ref, decays_ref, raw_ref, sems):
    decays_ref[...] = jnp.full((8, HEAD), decay_ref[0, 0], F32)
    pairs = []
    for group in range(GROUPS):
        span = pl.ds(group * GROUP, GROUP)
        pairs.append((gate_up_hbm.at[span], raw_ref.at[span]))
    pairs.append((down_hbm, weights_ref.at[pl.ds(2 * UNITS, UNITS)]))
    copies = started(pairs, sems)
    for group in range(GROUPS):
        copies[group].wait()

        @pl.loop(0, GROUP // 16)
        def _(part):
            raw = raw_ref[pl.ds(group * GROUP + part * 16, 16)]
            target = pl.ds(pl.multiple_of(2 * group * GROUP + part * 32, 32), 32)
            weights_ref[target] = raw.reshape(32, DIM)

    copies[GROUPS].wait()


def finish_kernel(parts_ref, mixed_ref, out_ref):
    for half in range(2):
        place = slice(half * HALF, (half + 1) * HALF)
        total = mixed_ref[place].astype(F32)
        for chip in range(BLOCKS // 2):
            total = total + parts_ref[half * (BLOCKS // 2) + chip].astype(F32)
        out_ref[place] = total.astype(BF16)


def shape_of(*shape, dtype=BF16):
    return jax.ShapeDtypeStruct(shape, dtype)


def local_call(kernel, outs, ins, scratch=(), spaces=None, out_space=pltpu.VMEM, cost=None, mib=8):
    spaces = spaces or {}
    ins = [
        pltpu.with_memory_space_constraint(value, spaces[i])
        if spaces.get(i) in (pltpu.HBM, pltpu.VMEM)
        else value
        for i, value in enumerate(ins)
    ]
    return pl.pallas_call(
        kernel,
        out_shape=outs,
        in_specs=[pl.BlockSpec(memory_space=spaces.get(i, pltpu.VMEM)) for i in range(len(ins))],
        out_specs=jax.tree.map(lambda _: pl.BlockSpec(memory_space=out_space), outs),
        scratch_shapes=list(scratch),
        compiler_params=pltpu.CompilerParams(vmem_limit_bytes=mib << 20),
        cost_estimate=cost,
    )(*ins)


def swapped(value):
    return lax.ppermute(value, "core", [(0, 1), (1, 0)])


def exchanged(value, axes=PEERS):
    return lax.all_to_all(value, axes, 0, 0, tiled=True)


def per_device(
    arriving,
    entering,
    gain_attention,
    gain_key,
    decay_rate,
    state_in,
    gain_linear,
    gain_feed,
    gate_up,
    down_weight,
    prefix_keys,
    prefix_values,
    lengths,
):
    rows = arriving[0]
    sent = local_call(
        start_kernel,
        shape_of(SHARDS, 2 * ROWS + TAIL, HEAD),
        (rows, prefix_keys[0], prefix_values[0]),
        scratch=(
            pltpu.VMEM((TOK, HEAD), BF16),
            pltpu.VMEM((ROWS, SHARDS, HEAD), BF16),
            pltpu.VMEM((ROWS, SHARDS, HEAD), BF16),
            pltpu.VMEM((SHARDS, 2 * ROWS + TAIL, HEAD), BF16),
            pltpu.SemaphoreType.DMA((5,)),
        ),
        spaces=dict.fromkeys(range(3), pltpu.HBM),
        out_space=pltpu.HBM,
    )
    sent = exchanged(sent, ("x", "core"))
    weights, decays = local_call(
        prepare_kernel,
        (shape_of(3 * UNITS, DIM), shape_of(8, HEAD, dtype=F32)),
        (decay_rate, gate_up[0], down_weight[0]),
        scratch=(pltpu.VMEM((UNITS, 2, DIM), BF16), pltpu.SemaphoreType.DMA((GROUPS + 1,))),
        spaces={0: pltpu.SMEM, 1: pltpu.HBM, 2: pltpu.HBM},
        cost=pl.CostEstimate(flops=0, bytes_accessed=8 << 20, transcendentals=0),
        mib=16,
    )
    parts, prefix, rows, memory, consts = local_call(
        merge_kernel,
        (
            shape_of(4, 8, HEAD, dtype=F32),
            shape_of(SHARDS, 2 * ROWS, HEAD),
            shape_of(TOK, HEAD),
            shape_of(HEAD, HEAD, dtype=F32),
            shape_of(8, SHARDS * ROWS, dtype=F32),
        ),
        (
            decays,
            lengths,
            sent,
            rows,
            state_in[0, 0],
            gain_attention,
            gain_key,
            gain_linear,
        ),
        scratch=(
            pltpu.SMEM((1, SHARDS), jnp.int32),
            pltpu.VMEM((8, HEAD), F32),
            pltpu.VMEM((SHARDS, TAIL, HEAD), BF16),
            pltpu.VMEM((3, 1, HEAD), F32),
            pltpu.SemaphoreType.DMA((9,)),
        ),
        spaces=dict.fromkeys(range(8), pltpu.HBM),
    )
    parts, sent_weights = lax.optimization_barrier((parts, weights))
    far_weights = swapped(sent_weights)
    parts = exchanged(parts, "tp").reshape(BLOCKS, HEAD)
    size = lax.axis_size("section")
    onward = [(i, (i + 1) % size) for i in range(size)]
    past = ()
    arrived = []
    for tick in range(TICKS):
        if tick:
            rows, parts = local_call(
                later_squares_kernel,
                (shape_of(TOK, HEAD), shape_of(BLOCKS, HEAD, dtype=F32)),
                (passed, entering[tick - 1]),
            )
            parts = exchanged(parts)
        outs = (shape_of(BLOCKS, HALF, HEAD), shape_of(TOK, HEAD), shape_of(2, TOK, HEAD))
        state = shape_of(HEAD, HEAD, dtype=F32)
        kernel = functools.partial(attention_kernel, tick)
        ins = (parts, consts, prefix, rows, memory, *past)
        if tick == 0:
            spread, mixed, turn, memory = local_call(kernel, (*outs, state), ins)
        else:
            spread, mixed, turn = local_call(kernel, outs, ins)
            memory = local_call(memory_kernel, state, (consts, memory, turn))
        past = (turn,)
        spread = exchanged(spread)
        down = local_call(
            feed_kernel,
            shape_of(BLOCKS, HALF, HEAD),
            (spread, gain_feed, weights, far_weights),
            scratch=(pltpu.VMEM((2, 2 * UNITS, HALF), F32),),
            mib=16,
        )
        down = exchanged(down)
        finished = local_call(finish_kernel, shape_of(TOK, HEAD), (down, mixed))
        passed = lax.ppermute(finished, "section", onward)
        arrived.append(passed)
    return (jnp.stack(arrived)[:, None], memory[None, None])


def solution(mesh):
    shape = mesh.devices.shape
    split = jax.sharding.Mesh(
        mesh.devices.reshape(shape[0], shape[1] // 2, 2, shape[2]), ("section", "x", "core", "tp")
    )
    kv = ("x", "core")
    in_specs = (
        P("section", None, SECTION),
        P(None, None, SECTION),
        P("section", None),
        P("section", None),
        P("section", SECTION),
        P("section", SECTION, None, None),
        P("section", SECTION),
        P("section", None),
        P("section", SECTION, None, None),
        P("section", SECTION, None),
        P("section", kv, None, "tp"),
        P("section", kv, None, "tp"),
        P("section", None),
    )
    out_specs = (P(None, "section", None, SECTION), P("section", SECTION, None, None))
    return jax.shard_map(
        per_device, mesh=split, in_specs=in_specs, out_specs=out_specs, check_vma=False
    )
```

```python
import functools

import jax
import jax.numpy as jnp
from jax import lax
from jax.experimental import pallas as pl
from jax.experimental.pallas import tpu as pltpu
from jax.sharding import PartitionSpec as P

TICKS = 2
TOK = 128
HALF = 64
HEAD = 128
DIM = 4096
UNITS = 144
BLOCKS = 32
SHARDS = 8
ROWS = 64
TAIL = 16
GROUPS = 3
GROUP = UNITS // GROUPS
EPS = 1e-6
MASKED = -1e30
SECTION = ("x", "core", "tp")
PEERS = ("core", "x", "tp")
F32 = jnp.float32
BF16 = jnp.bfloat16
HIGH = lax.Precision.HIGHEST


def dot(left, right, dims, precision=None):
    return lax.dot_general(
        left, right, ((dims[:1], dims[1:]), ((), ())), precision=precision, preferred_element_type=F32
    )


def peer(block):
    return block // 4 % 2 * 16 + block // 8 * 4 + block % 4


def pieces(value, count, axis):
    parts = []
    for _ in range(count):
        parts.append(value.astype(BF16))
        value = value - parts[-1].astype(F32)
    return jnp.concatenate(parts, axis=axis)


def lane_sums(values, count, rows):
    split = pieces(values, count, 1)
    return dot(jnp.ones((rows, split.shape[1]), BF16), split, (1, 1))


def block_place():
    return (lax.axis_index("x") * 2 + lax.axis_index("core")) * 4 + lax.axis_index("tp")


def write_square_sums(rows, parts_ref):
    squares = rows.astype(F32)
    squares = squares * squares
    sums = lane_sums(squares, 2, 8)
    parts_ref[...] = jnp.concatenate([sums] * (BLOCKS // 8), axis=0)


def started(pairs, sems):
    copies = [pltpu.make_async_copy(*pair, sems.at[i]) for i, pair in enumerate(pairs)]
    for copy in copies:
        copy.start()
    return copies


def start_kernel(rows_hbm, keys_hbm, values_hbm, out_hbm, rows_ref, keys_ref, values_ref, out_ref, sems):
    copies = started(
        [(rows_hbm, rows_ref), (keys_hbm, keys_ref), (values_hbm, values_ref)], sems
    )
    copies[0].wait()
    squares = rows_ref[...].astype(F32)
    squares = squares * squares
    sums = lane_sums(squares, 2, TAIL)
    high = sums.astype(BF16).astype(F32)
    middle = (sums - high).astype(BF16).astype(F32)
    row = lax.broadcasted_iota(jnp.int32, (TAIL, HEAD), 0)
    tail = jnp.where(row == 2, sums - high - middle, 0.0)
    tail = jnp.where(row == 0, high, jnp.where(row == 1, middle, tail)).astype(BF16)
    for index, ref in enumerate((keys_ref, values_ref)):
        copies[1 + index].wait()
        by_head = jnp.swapaxes(ref[...], 0, 1)
        span = pl.ds(index * ROWS, ROWS)
        for shard in range(SHARDS):
            out_ref[shard, span] = by_head[shard % 4 * 2 + shard // 4]
            if index:
                out_ref[shard, 2 * ROWS :] = tail
        span = pl.ds(index * ROWS, ROWS + index * TAIL)
        copies.append(
            pltpu.make_async_copy(out_ref.at[:, span], out_hbm.at[:, span], sems.at[3 + index])
        )
        copies[-1].start()
    for copy in copies[3:]:
        copy.wait()


def merge_kernel(
    decays_hbm,
    lengths_hbm,
    swapped_hbm,
    rows_hbm,
    memory_hbm,
    gain_hbm,
    key_gain_hbm,
    linear_gain_hbm,
    parts_ref,
    prefix_ref,
    rows_ref,
    memory_ref,
    consts_ref,
    lengths_ref,
    decays_ref,
    tails_ref,
    gains_ref,
    sems,
):
    place = pl.ds(pl.multiple_of(block_place() * HEAD, HEAD), HEAD)
    copies = started(
        [
            (swapped_hbm.at[:, pl.ds(2 * ROWS, TAIL)], tails_ref),
            (lengths_hbm, lengths_ref),
            (decays_hbm, decays_ref),
            (gain_hbm.at[:, place], gains_ref.at[0]),
            (key_gain_hbm.at[:, place], gains_ref.at[1]),
            (linear_gain_hbm, gains_ref.at[2]),
            (rows_hbm, rows_ref),
            (memory_hbm, memory_ref),
            (swapped_hbm.at[:, pl.ds(0, 2 * ROWS)], prefix_ref),
        ],
        sems,
    )
    copies[0].wait()
    tails = tails_ref[0].astype(F32)
    for shard in range(1, SHARDS):
        tails = tails + tails_ref[shard].astype(F32)
    sums = jnp.sum(tails, axis=0, keepdims=True) * (1.0 / 8)
    for target in range(4):
        parts_ref[target] = jnp.broadcast_to(sums, (8, HEAD))
    for copy in copies[1:]:
        copy.wait()
    slot = lax.broadcasted_iota(jnp.int32, (1, SHARDS * ROWS), 1)
    used = jnp.zeros((1, SHARDS * ROWS), jnp.int32)
    for shard in range(SHARDS):
        length = lengths_ref[0, shard % 4 * 2 + shard // 4]
        used = jnp.where(slot // ROWS == shard, length, used)
    consts_ref[0:1] = jnp.where(slot % ROWS < used, 0.0, MASKED)
    for index in range(3):
        consts_ref[1:2, index * HEAD : (index + 1) * HEAD] = gains_ref[index]
    consts_ref[1:2, 3 * HEAD :] = decays_ref[0:1]


def later_squares_kernel(passed_ref, entering_ref, rows_ref, parts_ref):
    rows = jnp.where(lax.axis_index("section") == 0, entering_ref[...], passed_ref[...])
    rows_ref[...] = rows
    write_square_sums(rows, parts_ref)


def memory_kernel(consts_ref, memory_ref, turn_ref, out_ref):
    decay = consts_ref[1:2, 3 * HEAD :]
    row = lax.broadcasted_iota(jnp.int32, (TOK, HEAD), 0).astype(F32)
    tail = turn_ref[0].astype(F32) * jnp.exp(-decay * (TOK - 1.0 - row))
    update = dot(tail, turn_ref[1].astype(F32), (0, 0), HIGH) * HEAD**-0.5
    out_ref[...] = memory_ref[...] * jnp.exp(-decay * TOK) + update


def attention_kernel(
    tick, parts_ref, consts_ref, prefix_ref, rows_ref, memory_ref, *refs
):
    scale = HEAD**-0.5
    if tick:
        past_ref, *refs = refs
    spread_ref, mixed_ref, turn_ref = refs[:3]
    barred = consts_ref[0:1]
    gain, key_gain, linear_gain, decay = [
        consts_ref[1:2, index * HEAD : (index + 1) * HEAD] for index in range(4)
    ]
    parts = pieces(parts_ref[...], 3, 0)
    sums = dot(parts, jnp.ones(parts.shape, BF16), (0, 0))
    rows = rows_ref[...].astype(F32)
    normed = rows * lax.rsqrt(sums * (1.0 / DIM) + EPS) * gain
    queries = normed.astype(BF16)
    keys = (normed * key_gain).astype(BF16)
    turn_ref[0] = keys
    turn_ref[1] = queries
    if tick == 0:
        memory_kernel(consts_ref, memory_ref, turn_ref, refs[3])

    shape = (TOK, TOK)
    row = lax.broadcasted_iota(jnp.int32, shape, 0)
    column = lax.broadcasted_iota(jnp.int32, shape, 1)
    causal = column <= row
    own_scores = dot(queries, keys, (1, 1)) * scale
    age = jnp.where(causal, row - column, 0).astype(F32)
    weights = jnp.where(causal, own_scores * jnp.exp(-decay * age), 0.0).astype(BF16)
    row = row.astype(F32)
    memory = memory_ref[...]
    wide = queries.astype(F32)
    raw = dot(weights, queries, (1, 0)) + dot(wide, memory, (1, 0), HIGH) * jnp.exp(
        -decay * (row + 1.0)
    )
    spread = jnp.mean(raw * raw, axis=1, keepdims=True)
    linear = raw * lax.rsqrt(spread + EPS) * linear_gain

    prefix_keys = prefix_ref[:, :ROWS, :].reshape(SHARDS * ROWS, HEAD)
    prefix_values = prefix_ref[:, ROWS:, :].reshape(SHARDS * ROWS, HEAD)
    prefix_scores = dot(queries, prefix_keys, (1, 1)) * scale + barred
    groups = [
        (prefix_scores, prefix_values),
        (jnp.where(causal, own_scores, MASKED), queries),
    ]
    if tick:
        groups.append((dot(queries, past_ref[0], (1, 1)) * scale, past_ref[1]))
    top = functools.reduce(
        jnp.maximum, [jnp.max(scores, axis=1, keepdims=True) for scores, _ in groups]
    )
    total = 0.0
    weighted = 0.0
    for scores, values in groups:
        probabilities = jnp.exp(scores - top)
        total = total + jnp.sum(probabilities, axis=1, keepdims=True)
        weighted = weighted + dot(probabilities.astype(BF16), values, (1, 0))
    mixed = (rows + (linear + weighted / total)).astype(BF16)
    mixed_ref[...] = mixed
    for block in range(BLOCKS):
        half = block // 4 % 2
        spread_ref[peer(block)] = mixed[half * HALF : (half + 1) * HALF]


def feed_kernel(rows_ref, gain_ref, near_ref, far_ref, out_ref, wide_ref):
    step = 1024
    squares = jnp.zeros((HALF, HEAD), F32)
    sums = [0.0, 0.0]
    for first in range(0, DIM, step):
        place = slice(first, first + step)
        pieces = []
        for block in range(first // HEAD, (first + step) // HEAD):
            rows = rows_ref[peer(block)].astype(F32)
            squares = squares + rows * rows
            gain = gain_ref[:, block * HEAD : (block + 1) * HEAD]
            pieces.append((rows * gain).astype(BF16))
        feed = jnp.concatenate(pieces, axis=1)
        for side, ref in enumerate((near_ref, far_ref)):
            sums[side] = sums[side] + dot(ref[: 2 * UNITS, place], feed, (1, 1))
    mean = lane_sums(squares, 3, 8)[:1] * (1.0 / DIM)
    factor = lax.rsqrt(mean + EPS)
    hidden = []
    for side in range(2):
        wide_ref[side] = sums[side]
        gate = wide_ref[side, pl.ds(0, UNITS, stride=2), :] * factor
        up = wide_ref[side, pl.ds(1, UNITS, stride=2), :] * factor
        hidden.append(jnp.transpose((gate / (1.0 + jnp.exp(-gate)) * up).astype(BF16)))
    for first in range(0, DIM, step):
        place = slice(first, first + step)
        down = dot(hidden[0], near_ref[2 * UNITS :, place], (1, 0)) + dot(
            hidden[1], far_ref[2 * UNITS :, place], (1, 0)
        )
        for block in range(step // HEAD):
            out_ref[peer(first // HEAD + block)] = down[:, block * HEAD : (block + 1) * HEAD].astype(BF16)


def prepare_kernel(decay_ref, gate_up_hbm, down_hbm, weights_ref, decays_ref, raw_ref, sems):
    decays_ref[...] = jnp.full((8, HEAD), decay_ref[0, 0], F32)
    pairs = []
    for group in range(GROUPS):
        span = pl.ds(group * GROUP, GROUP)
        pairs.append((gate_up_hbm.at[span], raw_ref.at[span]))
    pairs.append((down_hbm, weights_ref.at[pl.ds(2 * UNITS, UNITS)]))
    copies = started(pairs, sems)
    for group in range(GROUPS):
        copies[group].wait()

        @pl.loop(0, GROUP // 16)
        def _(part):
            raw = raw_ref[pl.ds(group * GROUP + part * 16, 16)]
            target = pl.ds(pl.multiple_of(2 * group * GROUP + part * 32, 32), 32)
            weights_ref[target] = raw.reshape(32, DIM)

    copies[GROUPS].wait()


def finish_kernel(parts_ref, mixed_ref, out_ref):
    for half in range(2):
        place = slice(half * HALF, (half + 1) * HALF)
        total = mixed_ref[place].astype(F32)
        for chip in range(BLOCKS // 2):
            total = total + parts_ref[half * (BLOCKS // 2) + chip].astype(F32)
        out_ref[place] = total.astype(BF16)


def shape_of(*shape, dtype=BF16):
    return jax.ShapeDtypeStruct(shape, dtype)


def local_call(kernel, outs, ins, scratch=(), spaces=None, out_space=pltpu.VMEM, cost=None, mib=8):
    spaces = spaces or {}
    ins = [
        pltpu.with_memory_space_constraint(value, spaces[i])
        if spaces.get(i) in (pltpu.HBM, pltpu.VMEM)
        else value
        for i, value in enumerate(ins)
    ]
    return pl.pallas_call(
        kernel,
        out_shape=outs,
        in_specs=[pl.BlockSpec(memory_space=spaces.get(i, pltpu.VMEM)) for i in range(len(ins))],
        out_specs=jax.tree.map(lambda _: pl.BlockSpec(memory_space=out_space), outs),
        scratch_shapes=list(scratch),
        compiler_params=pltpu.CompilerParams(vmem_limit_bytes=mib << 20),
        cost_estimate=cost,
    )(*ins)


def swapped(value):
    return lax.ppermute(value, "core", [(0, 1), (1, 0)])


def exchanged(value, axes=PEERS):
    return lax.all_to_all(value, axes, 0, 0, tiled=True)


def per_device(
    arriving,
    entering,
    gain_attention,
    gain_key,
    decay_rate,
    state_in,
    gain_linear,
    gain_feed,
    gate_up,
    down_weight,
    prefix_keys,
    prefix_values,
    lengths,
):
    rows = arriving[0]
    sent = local_call(
        start_kernel,
        shape_of(SHARDS, 2 * ROWS + TAIL, HEAD),
        (rows, prefix_keys[0], prefix_values[0]),
        scratch=(
            pltpu.VMEM((TOK, HEAD), BF16),
            pltpu.VMEM((ROWS, SHARDS, HEAD), BF16),
            pltpu.VMEM((ROWS, SHARDS, HEAD), BF16),
            pltpu.VMEM((SHARDS, 2 * ROWS + TAIL, HEAD), BF16),
            pltpu.SemaphoreType.DMA((5,)),
        ),
        spaces=dict.fromkeys(range(3), pltpu.HBM),
        out_space=pltpu.HBM,
    )
    sent = exchanged(sent, ("core", "x"))
    weights, decays = local_call(
        prepare_kernel,
        (shape_of(3 * UNITS, DIM), shape_of(8, HEAD, dtype=F32)),
        (decay_rate, gate_up[0], down_weight[0]),
        scratch=(pltpu.VMEM((UNITS, 2, DIM), BF16), pltpu.SemaphoreType.DMA((GROUPS + 1,))),
        spaces={0: pltpu.SMEM, 1: pltpu.HBM, 2: pltpu.HBM},
        cost=pl.CostEstimate(flops=0, bytes_accessed=8 << 20, transcendentals=0),
        mib=16,
    )
    parts, prefix, rows, memory, consts = local_call(
        merge_kernel,
        (
            shape_of(4, 8, HEAD, dtype=F32),
            shape_of(SHARDS, 2 * ROWS, HEAD),
            shape_of(TOK, HEAD),
            shape_of(HEAD, HEAD, dtype=F32),
            shape_of(8, SHARDS * ROWS, dtype=F32),
        ),
        (
            decays,
            lengths,
            sent,
            rows,
            state_in[0, 0],
            gain_attention,
            gain_key,
            gain_linear,
        ),
        scratch=(
            pltpu.SMEM((1, SHARDS), jnp.int32),
            pltpu.VMEM((8, HEAD), F32),
            pltpu.VMEM((SHARDS, TAIL, HEAD), BF16),
            pltpu.VMEM((3, 1, HEAD), F32),
            pltpu.SemaphoreType.DMA((9,)),
        ),
        spaces=dict.fromkeys(range(8), pltpu.HBM),
    )
    parts, sent_weights = lax.optimization_barrier((parts, weights))
    far_weights = swapped(sent_weights)
    parts = exchanged(parts, "tp").reshape(BLOCKS, HEAD)
    size = lax.axis_size("section")
    onward = [(i, (i + 1) % size) for i in range(size)]
    past = ()
    arrived = []
    for tick in range(TICKS):
        if tick:
            rows, parts = local_call(
                later_squares_kernel,
                (shape_of(TOK, HEAD), shape_of(BLOCKS, HEAD, dtype=F32)),
                (passed, entering[tick - 1]),
            )
            parts = exchanged(parts)
        outs = (shape_of(BLOCKS, HALF, HEAD), shape_of(TOK, HEAD), shape_of(2, TOK, HEAD))
        state = shape_of(HEAD, HEAD, dtype=F32)
        kernel = functools.partial(attention_kernel, tick)
        ins = (parts, consts, prefix, rows, memory, *past)
        if tick == 0:
            spread, mixed, turn, memory = local_call(kernel, (*outs, state), ins)
        else:
            spread, mixed, turn = local_call(kernel, outs, ins)
            memory = local_call(memory_kernel, state, (consts, memory, turn))
        past = (turn,)
        spread = exchanged(spread)
        down = local_call(
            feed_kernel,
            shape_of(BLOCKS, HALF, HEAD),
            (spread, gain_feed, weights, far_weights),
            scratch=(pltpu.VMEM((2, 2 * UNITS, HALF), F32),),
            mib=16,
        )
        down = exchanged(down)
        finished = local_call(finish_kernel, shape_of(TOK, HEAD), (down, mixed))
        passed = lax.ppermute(finished, "section", onward)
        arrived.append(passed)
    return (jnp.stack(arrived)[:, None], memory[None, None])


def solution(mesh):
    shape = mesh.devices.shape
    split = jax.sharding.Mesh(
        mesh.devices.reshape(shape[0], shape[1] // 2, 2, shape[2]), ("section", "x", "core", "tp")
    )
    kv = ("x", "core")
    in_specs = (
        P("section", None, SECTION),
        P(None, None, SECTION),
        P("section", None),
        P("section", None),
        P("section", SECTION),
        P("section", SECTION, None, None),
        P("section", SECTION),
        P("section", None),
        P("section", SECTION, None, None),
        P("section", SECTION, None),
        P("section", kv, None, "tp"),
        P("section", kv, None, "tp"),
        P("section", None),
    )
    out_specs = (P(None, "section", None, SECTION), P("section", SECTION, None, None))
    return jax.shard_map(
        per_device, mesh=split, in_specs=in_specs, out_specs=out_specs, check_vma=False
    )
```

```python
import functools

import jax
import jax.numpy as jnp
from jax import lax
from jax.experimental import pallas as pl
from jax.experimental.pallas import tpu as pltpu
from jax.sharding import PartitionSpec as P

TICKS = 2
TOK = 128
HALF = 64
HEAD = 128
DIM = 4096
UNITS = 144
BLOCKS = 32
SHARDS = 8
ROWS = 64
TAIL = 16
GROUPS = 3
GROUP = UNITS // GROUPS
EPS = 1e-6
MASKED = -1e30
SECTION = ("x", "core", "tp")
PEERS = ("core", "x", "tp")
F32 = jnp.float32
BF16 = jnp.bfloat16


def dot(left, right, dims):
    return lax.dot_general(
        left, right, ((dims[:1], dims[1:]), ((), ())), preferred_element_type=F32
    )


def peer(block):
    return block // 4 % 2 * 16 + block // 8 * 4 + block % 4


def pieces(value, count, axis):
    parts = []
    for _ in range(count):
        parts.append(value.astype(BF16))
        value = value - parts[-1].astype(F32)
    return jnp.concatenate(parts, axis=axis)


def lane_sums(values, count, rows):
    split = pieces(values, count, 1)
    return dot(jnp.ones((rows, split.shape[1]), BF16), split, (1, 1))


def block_place():
    return (lax.axis_index("x") * 2 + lax.axis_index("core")) * 4 + lax.axis_index("tp")


def write_square_sums(rows, parts_ref):
    squares = rows.astype(F32)
    squares = squares * squares
    sums = lane_sums(squares, 2, 8)
    parts_ref[...] = jnp.concatenate([sums] * (BLOCKS // 8), axis=0)


def started(pairs, sems):
    copies = [pltpu.make_async_copy(*pair, sems.at[i]) for i, pair in enumerate(pairs)]
    for copy in copies:
        copy.start()
    return copies


def start_kernel(rows_hbm, keys_hbm, values_hbm, out_hbm, rows_ref, keys_ref, values_ref, out_ref, sems):
    copies = started(
        [(rows_hbm, rows_ref), (keys_hbm, keys_ref), (values_hbm, values_ref)], sems
    )
    copies[0].wait()
    squares = rows_ref[...].astype(F32)
    squares = squares * squares
    sums = lane_sums(squares, 2, TAIL)
    high = sums.astype(BF16).astype(F32)
    middle = (sums - high).astype(BF16).astype(F32)
    row = lax.broadcasted_iota(jnp.int32, (TAIL, HEAD), 0)
    tail = jnp.where(row == 2, sums - high - middle, 0.0)
    tail = jnp.where(row == 0, high, jnp.where(row == 1, middle, tail)).astype(BF16)
    for index, ref in enumerate((keys_ref, values_ref)):
        copies[1 + index].wait()
        by_head = jnp.swapaxes(ref[...], 0, 1)
        span = pl.ds(index * ROWS, ROWS)
        for shard in range(SHARDS):
            out_ref[shard, span] = by_head[shard % 4 * 2 + shard // 4]
            if index:
                out_ref[shard, 2 * ROWS :] = tail
        span = pl.ds(index * ROWS, ROWS + index * TAIL)
        copies.append(
            pltpu.make_async_copy(out_ref.at[:, span], out_hbm.at[:, span], sems.at[3 + index])
        )
        copies[-1].start()
    for copy in copies[3:]:
        copy.wait()


def merge_kernel(
    decays_hbm,
    lengths_hbm,
    swapped_hbm,
    rows_hbm,
    memory_hbm,
    gain_hbm,
    key_gain_hbm,
    linear_gain_hbm,
    parts_ref,
    prefix_ref,
    rows_ref,
    memory_ref,
    consts_ref,
    lengths_ref,
    decays_ref,
    tails_ref,
    gains_ref,
    sems,
):
    place = pl.ds(pl.multiple_of(block_place() * HEAD, HEAD), HEAD)
    copies = started(
        [
            (swapped_hbm.at[:, pl.ds(2 * ROWS, TAIL)], tails_ref),
            (lengths_hbm, lengths_ref),
            (decays_hbm, decays_ref),
            (gain_hbm.at[:, place], gains_ref.at[0]),
            (key_gain_hbm.at[:, place], gains_ref.at[1]),
            (linear_gain_hbm, gains_ref.at[2]),
            (rows_hbm, rows_ref),
            (memory_hbm, memory_ref),
            (swapped_hbm.at[:, pl.ds(0, 2 * ROWS)], prefix_ref),
        ],
        sems,
    )
    copies[0].wait()
    tails = tails_ref[0].astype(F32)
    for shard in range(1, SHARDS):
        tails = tails + tails_ref[shard].astype(F32)
    sums = jnp.sum(tails, axis=0, keepdims=True) * (1.0 / 8)
    for target in range(4):
        parts_ref[target] = jnp.broadcast_to(sums, (8, HEAD))
    for copy in copies[1:]:
        copy.wait()
    slot = lax.broadcasted_iota(jnp.int32, (1, SHARDS * ROWS), 1)
    used = jnp.zeros((1, SHARDS * ROWS), jnp.int32)
    for shard in range(SHARDS):
        length = lengths_ref[0, shard % 4 * 2 + shard // 4]
        used = jnp.where(slot // ROWS == shard, length, used)
    consts_ref[0:1] = jnp.where(slot % ROWS < used, 0.0, MASKED)
    for index in range(3):
        consts_ref[1:2, index * HEAD : (index + 1) * HEAD] = gains_ref[index]
    consts_ref[1:2, 3 * HEAD :] = decays_ref[0:1]


def later_squares_kernel(passed_ref, entering_ref, rows_ref, parts_ref):
    rows = jnp.where(lax.axis_index("section") == 0, entering_ref[...], passed_ref[...])
    rows_ref[...] = rows
    write_square_sums(rows, parts_ref)


def memory_kernel(consts_ref, memory_ref, turn_ref, out_ref):
    decay = consts_ref[1:2, 3 * HEAD :]
    row = lax.broadcasted_iota(jnp.int32, (TOK, HEAD), 0).astype(F32)
    tail = turn_ref[0].astype(F32) * jnp.exp(-decay * (TOK - 1.0 - row))
    queries = jnp.concatenate([turn_ref[1]] * 3, axis=0)
    update = dot(pieces(tail, 3, 0), queries, (0, 0)) * HEAD**-0.5
    out_ref[...] = memory_ref[...] * jnp.exp(-decay * TOK) + update


def attention_kernel(
    tick, parts_ref, consts_ref, prefix_ref, rows_ref, memory_ref, *refs
):
    scale = HEAD**-0.5
    if tick:
        past_ref, *refs = refs
    spread_ref, mixed_ref, turn_ref = refs[:3]
    barred = consts_ref[0:1]
    gain, key_gain, linear_gain, decay = [
        consts_ref[1:2, index * HEAD : (index + 1) * HEAD] for index in range(4)
    ]
    parts = pieces(parts_ref[...], 3, 0)
    sums = dot(parts, jnp.ones(parts.shape, BF16), (0, 0))
    rows = rows_ref[...].astype(F32)
    normed = rows * lax.rsqrt(sums * (1.0 / DIM) + EPS) * gain
    queries = normed.astype(BF16)
    keys = (normed * key_gain).astype(BF16)
    turn_ref[0] = keys
    turn_ref[1] = queries
    if tick == 0:
        memory_kernel(consts_ref, memory_ref, turn_ref, refs[3])

    shape = (TOK, TOK)
    row = lax.broadcasted_iota(jnp.int32, shape, 0)
    column = lax.broadcasted_iota(jnp.int32, shape, 1)
    causal = column <= row
    own_scores = dot(queries, keys, (1, 1)) * scale
    age = jnp.where(causal, row - column, 0).astype(F32)
    weights = jnp.where(causal, own_scores * jnp.exp(-decay * age), 0.0).astype(BF16)
    row = row.astype(F32)
    memory = memory_ref[...]
    raw = dot(weights, queries, (1, 0)) + dot(jnp.concatenate([queries] * 3, axis=1), pieces(memory, 3, 0), (1, 0)) * jnp.exp(
        -decay * (row + 1.0)
    )
    spread = jnp.mean(raw * raw, axis=1, keepdims=True)
    linear = raw * lax.rsqrt(spread + EPS) * linear_gain

    prefix_keys = prefix_ref[:, :ROWS, :].reshape(SHARDS * ROWS, HEAD)
    prefix_values = prefix_ref[:, ROWS:, :].reshape(SHARDS * ROWS, HEAD)
    prefix_scores = dot(queries, prefix_keys, (1, 1)) * scale + barred
    groups = [
        (prefix_scores, prefix_values),
        (jnp.where(causal, own_scores, MASKED), queries),
    ]
    if tick:
        groups.append((dot(queries, past_ref[0], (1, 1)) * scale, past_ref[1]))
    top = functools.reduce(
        jnp.maximum, [jnp.max(scores, axis=1, keepdims=True) for scores, _ in groups]
    )
    total = 0.0
    weighted = 0.0
    for scores, values in groups:
        probabilities = jnp.exp(scores - top)
        total = total + jnp.sum(probabilities, axis=1, keepdims=True)
        weighted = weighted + dot(probabilities.astype(BF16), values, (1, 0))
    mixed = (rows + (linear + weighted / total)).astype(BF16)
    mixed_ref[...] = mixed
    for block in range(BLOCKS):
        half = block // 4 % 2
        spread_ref[peer(block)] = mixed[half * HALF : (half + 1) * HALF]


def feed_kernel(rows_ref, gain_ref, near_ref, far_ref, out_ref, wide_ref):
    step = 1024
    squares = jnp.zeros((HALF, HEAD), F32)
    sums = [0.0, 0.0]
    for first in range(0, DIM, step):
        place = slice(first, first + step)
        pieces = []
        for block in range(first // HEAD, (first + step) // HEAD):
            rows = rows_ref[peer(block)].astype(F32)
            squares = squares + rows * rows
            gain = gain_ref[:, block * HEAD : (block + 1) * HEAD]
            pieces.append((rows * gain).astype(BF16))
        feed = jnp.concatenate(pieces, axis=1)
        for side, ref in enumerate((near_ref, far_ref)):
            sums[side] = sums[side] + dot(ref[: 2 * UNITS, place], feed, (1, 1))
    mean = lane_sums(squares, 3, 8)[:1] * (1.0 / DIM)
    factor = lax.rsqrt(mean + EPS)
    hidden = []
    for side in range(2):
        wide_ref[side] = sums[side]
        gate = wide_ref[side, pl.ds(0, UNITS, stride=2), :] * factor
        up = wide_ref[side, pl.ds(1, UNITS, stride=2), :] * factor
        hidden.append(jnp.transpose((gate / (1.0 + jnp.exp(-gate)) * up).astype(BF16)))
    for first in range(0, DIM, step):
        place = slice(first, first + step)
        down = dot(hidden[0], near_ref[2 * UNITS :, place], (1, 0)) + dot(
            hidden[1], far_ref[2 * UNITS :, place], (1, 0)
        )
        for block in range(step // HEAD):
            out_ref[peer(first // HEAD + block)] = down[:, block * HEAD : (block + 1) * HEAD].astype(BF16)


def prepare_kernel(decay_ref, gate_up_hbm, down_hbm, weights_ref, decays_ref, raw_ref, sems):
    decays_ref[...] = jnp.full((8, HEAD), decay_ref[0, 0], F32)
    pairs = []
    for group in range(GROUPS):
        span = pl.ds(group * GROUP, GROUP)
        pairs.append((gate_up_hbm.at[span], raw_ref.at[span]))
    pairs.append((down_hbm, weights_ref.at[pl.ds(2 * UNITS, UNITS)]))
    copies = started(pairs, sems)
    for group in range(GROUPS):
        copies[group].wait()

        @pl.loop(0, GROUP // 16)
        def _(part):
            raw = raw_ref[pl.ds(group * GROUP + part * 16, 16)]
            target = pl.ds(pl.multiple_of(2 * group * GROUP + part * 32, 32), 32)
            weights_ref[target] = raw.reshape(32, DIM)

    copies[GROUPS].wait()


def finish_kernel(parts_ref, mixed_ref, out_ref):
    for half in range(2):
        place = slice(half * HALF, (half + 1) * HALF)
        total = mixed_ref[place].astype(F32)
        for chip in range(BLOCKS // 2):
            total = total + parts_ref[half * (BLOCKS // 2) + chip].astype(F32)
        out_ref[place] = total.astype(BF16)


def shape_of(*shape, dtype=BF16):
    return jax.ShapeDtypeStruct(shape, dtype)


def local_call(kernel, outs, ins, scratch=(), spaces=None, out_space=pltpu.VMEM, cost=None, mib=8):
    spaces = spaces or {}
    ins = [
        pltpu.with_memory_space_constraint(value, spaces[i])
        if spaces.get(i) in (pltpu.HBM, pltpu.VMEM)
        else value
        for i, value in enumerate(ins)
    ]
    return pl.pallas_call(
        kernel,
        out_shape=outs,
        in_specs=[pl.BlockSpec(memory_space=spaces.get(i, pltpu.VMEM)) for i in range(len(ins))],
        out_specs=jax.tree.map(lambda _: pl.BlockSpec(memory_space=out_space), outs),
        scratch_shapes=list(scratch),
        compiler_params=pltpu.CompilerParams(vmem_limit_bytes=mib << 20),
        cost_estimate=cost,
    )(*ins)


def swapped(value):
    return lax.ppermute(value, "core", [(0, 1), (1, 0)])


def exchanged(value, axes=PEERS):
    return lax.all_to_all(value, axes, 0, 0, tiled=True)


def per_device(
    arriving,
    entering,
    gain_attention,
    gain_key,
    decay_rate,
    state_in,
    gain_linear,
    gain_feed,
    gate_up,
    down_weight,
    prefix_keys,
    prefix_values,
    lengths,
):
    rows = arriving[0]
    sent = local_call(
        start_kernel,
        shape_of(SHARDS, 2 * ROWS + TAIL, HEAD),
        (rows, prefix_keys[0], prefix_values[0]),
        scratch=(
            pltpu.VMEM((TOK, HEAD), BF16),
            pltpu.VMEM((ROWS, SHARDS, HEAD), BF16),
            pltpu.VMEM((ROWS, SHARDS, HEAD), BF16),
            pltpu.VMEM((SHARDS, 2 * ROWS + TAIL, HEAD), BF16),
            pltpu.SemaphoreType.DMA((5,)),
        ),
        spaces=dict.fromkeys(range(3), pltpu.HBM),
        out_space=pltpu.HBM,
    )
    sent = exchanged(sent, ("core", "x"))
    weights, decays = local_call(
        prepare_kernel,
        (shape_of(3 * UNITS, DIM), shape_of(8, HEAD, dtype=F32)),
        (decay_rate, gate_up[0], down_weight[0]),
        scratch=(pltpu.VMEM((UNITS, 2, DIM), BF16), pltpu.SemaphoreType.DMA((GROUPS + 1,))),
        spaces={0: pltpu.SMEM, 1: pltpu.HBM, 2: pltpu.HBM},
        cost=pl.CostEstimate(flops=0, bytes_accessed=8 << 20, transcendentals=0),
        mib=16,
    )
    parts, prefix, rows, memory, consts = local_call(
        merge_kernel,
        (
            shape_of(4, 8, HEAD, dtype=F32),
            shape_of(SHARDS, 2 * ROWS, HEAD),
            shape_of(TOK, HEAD),
            shape_of(HEAD, HEAD, dtype=F32),
            shape_of(8, SHARDS * ROWS, dtype=F32),
        ),
        (
            decays,
            lengths,
            sent,
            rows,
            state_in[0, 0],
            gain_attention,
            gain_key,
            gain_linear,
        ),
        scratch=(
            pltpu.SMEM((1, SHARDS), jnp.int32),
            pltpu.VMEM((8, HEAD), F32),
            pltpu.VMEM((SHARDS, TAIL, HEAD), BF16),
            pltpu.VMEM((3, 1, HEAD), F32),
            pltpu.SemaphoreType.DMA((9,)),
        ),
        spaces=dict.fromkeys(range(8), pltpu.HBM),
    )
    parts, sent_weights = lax.optimization_barrier((parts, weights))
    far_weights = swapped(sent_weights)
    parts = exchanged(parts, "tp").reshape(BLOCKS, HEAD)
    size = lax.axis_size("section")
    onward = [(i, (i + 1) % size) for i in range(size)]
    past = ()
    arrived = []
    for tick in range(TICKS):
        if tick:
            rows, parts = local_call(
                later_squares_kernel,
                (shape_of(TOK, HEAD), shape_of(BLOCKS, HEAD, dtype=F32)),
                (passed, entering[tick - 1]),
            )
            parts = exchanged(parts)
        outs = (shape_of(BLOCKS, HALF, HEAD), shape_of(TOK, HEAD), shape_of(2, TOK, HEAD))
        state = shape_of(HEAD, HEAD, dtype=F32)
        kernel = functools.partial(attention_kernel, tick)
        ins = (parts, consts, prefix, rows, memory, *past)
        if tick == 0:
            spread, mixed, turn, memory = local_call(kernel, (*outs, state), ins)
        else:
            spread, mixed, turn = local_call(kernel, outs, ins)
            memory = local_call(memory_kernel, state, (consts, memory, turn))
        past = (turn,)
        spread = exchanged(spread)
        down = local_call(
            feed_kernel,
            shape_of(BLOCKS, HALF, HEAD),
            (spread, gain_feed, weights, far_weights),
            scratch=(pltpu.VMEM((2, 2 * UNITS, HALF), F32),),
            mib=16,
        )
        down = exchanged(down)
        finished = local_call(finish_kernel, shape_of(TOK, HEAD), (down, mixed))
        passed = lax.ppermute(finished, "section", onward)
        arrived.append(passed)
    return (jnp.stack(arrived)[:, None], memory[None, None])


def solution(mesh):
    shape = mesh.devices.shape
    split = jax.sharding.Mesh(
        mesh.devices.reshape(shape[0], shape[1] // 2, 2, shape[2]), ("section", "x", "core", "tp")
    )
    kv = ("x", "core")
    in_specs = (
        P("section", None, SECTION),
        P(None, None, SECTION),
        P("section", None),
        P("section", None),
        P("section", SECTION),
        P("section", SECTION, None, None),
        P("section", SECTION),
        P("section", None),
        P("section", SECTION, None, None),
        P("section", SECTION, None),
        P("section", kv, None, "tp"),
        P("section", kv, None, "tp"),
        P("section", None),
    )
    out_specs = (P(None, "section", None, SECTION), P("section", SECTION, None, None))
    return jax.shard_map(
        per_device, mesh=split, in_specs=in_specs, out_specs=out_specs, check_vma=False
    )
```
